128 devices in a mesh: along: 4 (over x_lo, core), cross: 32 (over z, x_hi, y).
Axes of the slice: x: 4 (x_hi: 2, x_lo: 2; x = x_hi * 2 + x_lo), y: 4, z: 4, core: 2. Of those that a mesh axis runs over, the one named last changes fastest.
Arguments:
- adjoint_state: float32 [4, 32, 128, 4, 512], P(None, 'along', 'cross'), may hold values from -6 to 6
- snapshot_store: float32 [8192, 3, 4, 512], P(('along', 'cross')), may hold values from -6 to 6
- dispatch_slot: int32 [8192], P(('along', 'cross')), may hold values from 0 to 63, as said below
- arrival_slot: int32 [32, 128], P('along', 'cross'), may hold values from -1 to 63, as said below
- mic_node: int32 [16384], P(('along', 'cross')), may hold values from 0 to 2047
- mic_residual: float32 [16384], P(('along', 'cross')), may hold values from -6 to 6
Outputs:
- adjoint_next: float32 [4, 32, 128, 4, 512], P(None, 'along', 'cross')
- kappa_gradient: float32 [32, 128, 4, 512], P('along', 'cross')
The draws below stay inside these ranges and needn't reach their ends.
Inputs may be any that keep to these rules, and one draw needn't show every extreme that they name: `dispatch_slot`: each device's 64 entries are a permutation of 0 to 63. `arrival_slot`: on each device exactly 16 of the 8 x 4 columns are active; their values are distinct positions h * 2 + s (h a cross index, s < 2); the others are -1. Some holder fills all 2 slots to each owner.
All inputs are finite; a program needn't handle non-finite values.
Results may differ from the reference program's by a relative error of at most 0.00007.
Values sent between devices are 32-bit elements; how exact they have to be, the bound alone decides.
No kernel may reach another device: no remote copies, remote signals or barrier semaphores. Data moves between devices by JAX's collectives and lax.ppermute only.
A program may use at most 256 MiB of HBM per device.

```python
from functools import partial
import jax
import jax.numpy as jnp
import numpy as np
from jax import lax

NODES = 512
EA = 8
EC = 4
EZ = 4
MICS = 128
ACT = 16
CAP = 2
SLOTS = 64
N_ALONG = 4
N_CROSS = 32


def draw_dispatch_slot(key, part):
    key = jax.random.fold_in(key, 5)
    ranking = jax.random.randint(key, (N_ALONG * N_CROSS, SLOTS), 0, 1 << 20) * SLOTS + jnp.arange(SLOTS, dtype=jnp.int32)
    return jnp.argsort(ranking, axis=-1, stable=True).astype(jnp.int32).reshape(-1)


def place_routes(spots, picks):
    return jnp.full((EA * EC,), -1, jnp.int32).at[spots].set(picks)


def draw_arrival_slot(key, part):
    key = jax.random.fold_in(key, 9)
    key_jitter, key_bias, key_favor, key_columns = jax.random.split(key, 4)
    position = jnp.arange(SLOTS, dtype=jnp.int32)
    holder_of = position // CAP
    jitter = jax.random.randint(key_jitter, (N_ALONG, N_CROSS, SLOTS), 0, 1024)
    holder_bias = jax.random.randint(key_bias, (N_ALONG, N_CROSS), 0, 3)
    favored = jax.random.randint(key_favor, (N_ALONG, N_CROSS), 0, N_CROSS)
    favored = favored.at[0, 0].set(N_CROSS - 1)
    ranking = jitter + 1024 * holder_bias[:, holder_of][:, None, :]
    ranking = jnp.where(holder_of[None, None, :] == favored[:, :, None], 0, ranking + 1)
    ranking = ranking * SLOTS + position
    chosen = jnp.argsort(ranking, axis=-1, stable=True)[..., :ACT].astype(jnp.int32)
    column_rank = jax.random.randint(key_columns, (N_ALONG, N_CROSS, EA * EC), 0, 1 << 20) * (EA * EC) + jnp.arange(EA * EC, dtype=jnp.int32)
    placed = jnp.argsort(column_rank, axis=-1, stable=True)[..., :ACT].astype(jnp.int32)
    arrival = jax.vmap(jax.vmap(place_routes))(placed, chosen)
    return arrival.reshape(N_ALONG, N_CROSS, EA, EC).transpose(0, 2, 1, 3).reshape(N_ALONG * EA, N_CROSS * EC)


def plant(drawn, own_key, least, top_value):
    index_at = [jax.random.randint(jax.random.fold_in(own_key, axis), (), 0, length) for axis, length in enumerate(drawn.shape)]
    main_axis = drawn.shape.index(max(drawn.shape))
    neighbour = index_at[:main_axis] + [(index_at[main_axis] + 1) % drawn.shape[main_axis]] + index_at[main_axis + 1:]
    return drawn.at[tuple(index_at)].set(least).at[tuple(neighbour)].set(top_value)


def block_scale(key, extent, shards, smallest, largest):
    def one(dim, shards_of):
        heights = jax.random.uniform(jax.random.fold_in(jax.random.fold_in(key, 6), dim), (shards_of,), jnp.float32, smallest / len(shards), largest / len(shards))
        return jnp.repeat(jnp.exp(heights), extent[dim] // shards_of).reshape((-1,) + (1,) * (len(extent) - dim - 1))

    factor_of = one(*shards[0])
    for cut in shards[1:]:
        factor_of = factor_of * one(*cut)
    return factor_of


def normal_values(rng, shape, scale, most, cuts=(), held_as=jnp.bfloat16):
    gain = block_scale(rng, shape, cuts, -0.22, 0.18) if cuts else 1.0
    result = jax.random.normal(rng, shape, jnp.float32) * scale * gain
    return jnp.minimum(jnp.maximum(result, -most), most).astype(held_as)


def setup_inputs(seed: int = 0) -> dict:
    key_list = jax.random.split(jax.random.key(seed), 7)
    adjoint_state = normal_values(key_list[0], (4, EA * N_ALONG, EC * N_CROSS, EZ, NODES), 1.0, 6.0, ((1, 4), (2, 32)), jnp.float32)
    snapshot_store = normal_values(key_list[1], (N_ALONG * N_CROSS * SLOTS, 3, EZ, NODES), 1.0, 6.0, ((0, 128),), jnp.float32)
    dispatch_slot = draw_dispatch_slot(jax.random.fold_in(key_list[6], 71), 0)
    arrival_slot = draw_arrival_slot(jax.random.fold_in(key_list[6], 71), 0)
    mic_node = plant(jax.random.randint(key_list[4], (N_ALONG * N_CROSS * MICS,), 0, EA * EC * 64), jax.random.fold_in(key_list[4], 1), 0, (EA * EC * 64) - 1).astype(jnp.int32)
    mic_residual = normal_values(key_list[5], (N_ALONG * N_CROSS * MICS,), 1.0, 6.0, ((0, 128),), jnp.float32)
    return {"adjoint_state": adjoint_state, "snapshot_store": snapshot_store, "dispatch_slot": dispatch_slot, "arrival_slot": arrival_slot, "mic_node": mic_node, "mic_residual": mic_residual}


MACH = 0.3
ALPHA = 1.3
LIFT_SCALE = 56.0
TIME_STEP = 0.004
SOURCE_GAIN = 50.0
PRECISE = lax.Precision.HIGHEST
LOBATTO_INNER = [-0.8717401485096066, -0.5917001814331423, -0.2092992179024789, 0.2092992179024789, 0.5917001814331423, 0.8717401485096066]


def legendre_seven(points):
    previous = points * 0.0 + 1.0
    current = points * 1.0
    for degree_index in range(1, 7):
        following = ((2 * degree_index + 1) * points * current - degree_index * previous) / (degree_index + 1)
        previous, current = current, following
    return current


def derivative_tables():
    degree = 7
    points = np.array([-1.0] + LOBATTO_INNER + [1.0])
    values = legendre_seven(points)
    differ = points[:, None] - points[None, :] + np.eye(degree + 1)
    matrix = (values[:, None] / values[None, :]) / differ
    matrix = matrix * (1.0 - np.eye(degree + 1))
    matrix[0, 0] = -degree * (degree + 1) / 4.0
    matrix[degree, degree] = degree * (degree + 1) / 4.0
    identity_8 = np.eye(8)
    identity_64 = np.eye(64)
    along_table = 2.0 * np.kron(matrix, identity_64)
    cross_table = 2.0 * np.kron(np.kron(identity_8, matrix), identity_8)
    vertical_table = 2.0 * np.kron(identity_64, matrix)
    return tuple(jnp.asarray(operator_table.T, dtype=jnp.float32) for operator_table in (along_table, cross_table, vertical_table))


def derivative(nodal_rows, operator_table):
    flat_rows = nodal_rows.reshape(-1, 512)
    return jnp.dot(flat_rows, operator_table, precision=PRECISE).reshape(nodal_rows.shape)


def volume_terms(adjoint, tables):
    slope_along = derivative(adjoint, tables[0])
    slope_cross = derivative(jnp.stack([adjoint[0], adjoint[2]]), tables[1])
    slope_vertical = derivative(jnp.stack([adjoint[0], adjoint[3]]), tables[2])
    return jnp.stack([
        MACH * slope_along[0] + slope_along[1] + slope_cross[1] + slope_vertical[1],
        MACH * slope_along[1] + slope_along[0],
        MACH * slope_along[2] + slope_cross[0],
        MACH * slope_along[3] + slope_vertical[0]])


def face_traces(adjoint):
    nodal = adjoint.reshape(adjoint.shape[:-1] + (8, 8, 8))
    return (nodal[..., 0, :, :], nodal[..., 7, :, :], nodal[..., :, 0, :], nodal[..., :, 7, :], nodal[..., :, :, 0], nodal[..., :, :, 7])


def jump_flux(difference, direction, sign):
    pressure = difference[0]
    along_vel = difference[1]
    cross_vel = difference[2]
    vertical_vel = difference[3]
    nothing = jnp.zeros_like(pressure)
    if direction == 0:
        normal = [MACH * pressure + along_vel, MACH * along_vel + pressure, MACH * cross_vel, MACH * vertical_vel]
    elif direction == 1:
        normal = [cross_vel, nothing, pressure, nothing]
    else:
        normal = [vertical_vel, nothing, nothing, pressure]
    return -0.5 * LIFT_SCALE * (sign * jnp.stack(normal) + ALPHA * difference)


def vertical_exteriors(bottom, upper):
    mirror = jnp.array([1.0, 1.0, 1.0, -1.0], dtype=jnp.float32).reshape(4, 1, 1, 1, 1, 1)
    beneath = jnp.concatenate([bottom[:, :, :, :1] * mirror, upper[:, :, :, :-1]], axis=3)
    overhead = jnp.concatenate([bottom[:, :, :, 1:], jnp.zeros_like(bottom[:, :, :, :1])], axis=3)
    return beneath, overhead


def adjoint_rate(adjoint, tables, outside):
    inside = face_traces(adjoint)
    tendency = volume_terms(adjoint, tables)
    nodal = tendency.reshape(adjoint.shape[:-1] + (8, 8, 8))
    nodal = nodal.at[..., 0, :, :].add(jump_flux(inside[0] - outside[0], 0, -1.0))
    nodal = nodal.at[..., 7, :, :].add(jump_flux(inside[1] - outside[1], 0, 1.0))
    nodal = nodal.at[..., :, 0, :].add(jump_flux(inside[2] - outside[2], 1, -1.0))
    nodal = nodal.at[..., :, 7, :].add(jump_flux(inside[3] - outside[3], 1, 1.0))
    nodal = nodal.at[..., :, :, 0].add(jump_flux(inside[4] - outside[4], 2, -1.0))
    nodal = nodal.at[..., :, :, 7].add(jump_flux(inside[5] - outside[5], 2, 1.0))
    return nodal.reshape(adjoint.shape)


def divergence(fields, tables):
    return derivative(fields[:, 0], tables[0]) + derivative(fields[:, 1], tables[1]) + derivative(fields[:, 2], tables[2])


def ground_sources(node_index, values, total_nodes):
    return jnp.zeros((total_nodes,), jnp.float32).at[node_index].add(values)


def reference(adjoint_state, snapshot_store, dispatch_slot, arrival_slot, mic_node, mic_residual):
    tables = derivative_tables()
    traces = face_traces(adjoint_state)
    edge_along = jnp.zeros_like(traces[1][:, :1])
    edge_cross = jnp.zeros_like(traces[3][:, :, :1])
    beneath, overhead = vertical_exteriors(traces[4], traces[5])
    outside = (
        jnp.concatenate([edge_along, traces[1][:, :-1]], axis=1),
        jnp.concatenate([traces[0][:, 1:], edge_along], axis=1),
        jnp.concatenate([edge_cross, traces[3][:, :, :-1]], axis=2),
        jnp.concatenate([traces[2][:, :, 1:], edge_cross], axis=2),
        beneath, overhead)
    updated = adjoint_state + TIME_STEP * adjoint_rate(adjoint_state, tables, outside)
    placer = partial(ground_sources, total_nodes=EA * EC * 64)
    sources = jax.vmap(placer)(mic_node.reshape(N_ALONG * N_CROSS, MICS), mic_residual.reshape(N_ALONG * N_CROSS, MICS))
    sources = sources.reshape(N_ALONG, N_CROSS, EA, EC, 64).transpose(0, 2, 1, 3, 4).reshape(N_ALONG * EA, N_CROSS * EC, 64)
    updated = updated.at[0, :, :, 0, 0::8].add(TIME_STEP * SOURCE_GAIN * sources)

    stored = snapshot_store.reshape(N_ALONG, N_CROSS, SLOTS, 3, EZ, 512)
    routes = dispatch_slot.reshape(N_ALONG, N_CROSS, SLOTS)
    arrival = arrival_slot.reshape(N_ALONG, EA, N_CROSS, EC)
    clipped = jnp.maximum(arrival, 0)
    holder = clipped // CAP
    within = clipped % CAP
    along_index = jnp.arange(N_ALONG, dtype=jnp.int32).reshape(N_ALONG, 1, 1, 1)
    owner_index = jnp.arange(N_CROSS, dtype=jnp.int32).reshape(1, 1, N_CROSS, 1)
    store_slot = routes[along_index, holder, owner_index * CAP + within]
    blocks = stored[along_index, holder, store_slot]
    spread = divergence(blocks.reshape(-1, 3, EZ, 512), tables).reshape(N_ALONG * EA, N_CROSS * EC, EZ, 512)
    active = (arrival >= 0).astype(jnp.float32).reshape(N_ALONG * EA, N_CROSS * EC, 1, 1)
    gradient = TIME_STEP * adjoint_state[0] * spread * active
    return updated, gradient
```

```python
import jax
import jax.numpy as jnp
import numpy as np
from jax import lax
from jax.experimental import pallas as pl
from jax.experimental.pallas import tpu as pltpu
from jax.sharding import PartitionSpec as P

MACH = 0.3
ALPHA = 1.3
LIFT_SCALE = 56.0
TIME_STEP = 0.004
SOURCE_GAIN = 50.0
HALF_LIFT = 0.5 * LIFT_SCALE
LOBATTO_INNER = [
    -0.8717401485096066,
    -0.5917001814331423,
    -0.2092992179024789,
    0.2092992179024789,
    0.5917001814331423,
    0.8717401485096066,
]
F32 = jnp.float32
BF16 = jnp.bfloat16
VMEM_BYTES = 24 * 1024 * 1024


def legendre_seven(points):
    previous = points * 0.0 + 1.0
    current = points * 1.0
    for degree_index in range(1, 7):
        following = ((2 * degree_index + 1) * points * current - degree_index * previous) / (
            degree_index + 1
        )
        previous, current = (current, following)
    return current


def high_low(table):
    table = table.astype(np.float32)
    high = table.astype(BF16)
    low = (table - high.astype(np.float32)).astype(BF16)
    return np.stack([high, low])


def derivative_tables():
    degree = 7
    points = np.array([-1.0] + LOBATTO_INNER + [1.0])
    values = legendre_seven(points)
    differ = points[:, None] - points[None, :] + np.eye(degree + 1)
    matrix = values[:, None] / values[None, :] / differ
    matrix = matrix * (1.0 - np.eye(degree + 1))
    matrix[0, 0] = -degree * (degree + 1) / 4.0
    matrix[degree, degree] = degree * (degree + 1) / 4.0
    along = 2.0 * np.kron(matrix, np.eye(64))
    cross = 2.0 * np.kron(np.kron(np.eye(4), matrix), np.eye(8))
    vertical = 2.0 * np.kron(np.eye(32), matrix)
    return high_low(along.T), high_low(np.concatenate([cross.T, vertical.T]))


def split(x):
    high = x.astype(BF16)
    return high, (x - high.astype(F32)).astype(BF16)


def product(high, low, table_high, table_low):
    def dot(a, b):
        return jnp.dot(a, b, preferred_element_type=F32)

    return dot(high, table_high) + (dot(low, table_high) + dot(high, table_low))


def lanes(shape):
    return lax.broadcasted_iota(jnp.int32, shape, len(shape) - 1)


def tile(t):
    return slice(128 * t, 128 * t + 128)


def holder_kernel(
    slot_ref, adj_ref, store_ref, gx_ref, gyz_ref,
    out_ref, last_along, first_along, last_cross, first_cross,
    stage, high, low,
):
    def gather(g, carry):
        rows = pl.ds(pl.multiple_of(g * 16, 16), 16)
        for m in range(4):
            slot = slot_ref[4 * g + m]
            for f in range(3):
                stage[f, g, 4 * m : 4 * m + 4, :] = store_ref[slot, f]
        for f in range(3):
            high[f, rows], low[f, rows] = split(stage[f, g])
        return carry

    lax.fori_loop(0, 16, gather, 0)
    for c in range(2):
        part = slice(256 * c, 256 * c + 256)
        total = product(high[0], low[0], gx_ref[0, :, part], gx_ref[1, :, part])
        for f in (1, 2):
            rows = slice(256 * (f - 1), 256 * f)
            total += product(high[f, :, part], low[f, :, part], gyz_ref[0, rows], gyz_ref[1, rows])
        out_ref[:, :, part] = total.reshape(32, 8, 256)
    for f in range(4):
        for c in range(4):
            last_along[f, 4 * c : 4 * c + 4, :] = adj_ref[f, 7, c, :, tile(3)]
            first_along[f, 4 * c : 4 * c + 4, :] = adj_ref[f, 0, c, :, tile(0)]
    j = (lanes((4, 128)) >> 3) & 7
    for f in range(4):
        for t in range(4):
            last = adj_ref[f, 0, 3, :, tile(t)]
            last = pltpu.roll(last, 72, 1)
            first = adj_ref[f, 0, 0, :, tile(t)]
            for a in range(1, 8):
                other = adj_ref[f, a, 3, :, tile(t)]
                last = jnp.where(j == a, pltpu.roll(other, (72 + 8 * a) % 128, 1), last)
                other = adj_ref[f, a, 0, :, tile(t)]
                first = jnp.where(j == a, pltpu.roll(other, 8 * a, 1), first)
            last_cross[f, :, tile(t)] = last
            first_cross[f, :, tile(t)] = first


def volume_kernel(
    node_ref, residual_ref, adj_ref, gx_ref, gyz_ref, out_ref, state, high, low, slope_x, slope_y, slope_z, ground
):
    order = (2, 0, 3, 1)
    row = {f: 128 * n for n, f in enumerate(order)}
    state[:, 0] = jnp.zeros((4, 16, 512), F32)
    state[:, 9] = jnp.zeros((4, 16, 512), F32)

    def load(a, carry):
        for f in range(4):
            for c in range(4):
                state[f, a + 1, 4 * c : 4 * c + 4, :] = adj_ref[f, a, c]
            rows = pl.ds(pl.multiple_of(row[f] + a * 16, 16), 16)
            high[rows], low[rows] = split(state[f, a + 1])
        return carry

    lax.fori_loop(0, 8, load, 0)
    for c in range(2):
        part = slice(256 * c, 256 * c + 256)
        slope_x[:, part] = product(high[...], low[...], gx_ref[0, :, part], gx_ref[1, :, part])
        slope_y[:, part] = product(
            high[0:256, part], low[0:256, part], gyz_ref[0, 0:256], gyz_ref[1, 0:256]
        )
        slope_z[:, part] = product(
            high[128:384, part], low[128:384, part], gyz_ref[0, 256:512], gyz_ref[1, 256:512]
        )

    node = node_ref[...]
    residual = residual_ref[...]
    target = lax.broadcasted_iota(jnp.int32, (128, 128), 0)
    spread = jnp.where(target == 4 * (node >> 6), residual, 0.0)
    place = lax.broadcasted_iota(jnp.int32, (512, 128), 0) == 8 * (node & 63)
    place = jnp.where(place, 1.0, 0.0).astype(BF16)
    ones, rest = split(spread)
    twos = (spread - ones.astype(F32) - rest.astype(F32)).astype(BF16)

    def match(a):
        return lax.dot_general(a, place, (((1,), (1,)), ((), ())), preferred_element_type=F32)

    ground[...] = match(ones) + (match(rest) + match(twos))

    lane = lanes((8, 128))
    sub = lax.broadcasted_iota(jnp.int32, (8, 128), 0)
    j = (lane >> 3) & 7
    k = lane & 7
    e = sub & 3
    odd = sub >= 4
    top_y = j == 7
    top_z = k == 7
    floor = e == 0
    ceiling = e == 3
    zero = jnp.zeros((8, 128), F32)
    sign_y = jnp.where(j == 0, HALF_LIFT, jnp.where(top_y, -HALF_LIFT, 0.0))
    size_y = jnp.where((j == 0) | top_y, -HALF_LIFT * ALPHA, 0.0)
    sign_z = jnp.where(k == 0, HALF_LIFT, jnp.where(top_z, -HALF_LIFT, 0.0))
    size_z = jnp.where((k == 0) | top_z, -HALF_LIFT * ALPHA, 0.0)

    def step(a, carry):
        for t in range(4):
            here = tile(t)
            q = [[state[f, a + 1, 8 * g : 8 * g + 8, here] for g in range(2)] for f in range(4)]
            dy = [[None] * 2 for _ in range(4)]
            dz = [[None] * 2 for _ in range(4)]
            dx = [[None] * 2 for _ in range(4)]
            for f in range(4):
                swap = [pltpu.roll(q[f][g], 4, 0) for g in range(2)]
                before = [jnp.where(odd, swap[0], zero), jnp.where(odd, swap[1], swap[0])]
                after = [jnp.where(odd, swap[1], swap[0]), jnp.where(odd, zero, swap[1])]
                for g in range(2):
                    x = q[f][g]
                    outer = jnp.where(top_y, pltpu.roll(after[g], 56, 1), pltpu.roll(before[g], 72, 1))
                    dy[f][g] = x - outer
                    below = pltpu.roll(pltpu.roll(x, 1, 0), 121, 1)
                    below = jnp.where(floor, -x if f == 3 else x, below)
                    above = pltpu.roll(pltpu.roll(x, 7, 0), 7, 1)
                    above = jnp.where(ceiling, zero, above)
                    dz[f][g] = x - jnp.where(top_z, above, below)
                    if t == 0:
                        outer = pltpu.roll(state[f, a, 8 * g : 8 * g + 8, tile(3)], 64, 1)
                        dx[f][g] = jnp.where(lane < 64, x - outer, zero)
                    if t == 3:
                        outer = pltpu.roll(state[f, a + 2, 8 * g : 8 * g + 8, tile(0)], 64, 1)
                        dx[f][g] = jnp.where(lane >= 64, x - outer, zero)
            for g in range(2):
                def rows(f, base=0):
                    return pl.ds(pl.multiple_of(row[f] - base + a * 16 + 8 * g, 8), 8)

                gx = [slope_x[rows(f), here] for f in range(4)]
                gy = {f: slope_y[rows(f), here] for f in (2, 0)}
                gz = {f: slope_z[rows(f, 128), here] for f in (0, 3)}
                rate = [
                    MACH * gx[0] + gx[1] + gy[2] + gz[3],
                    MACH * gx[1] + gx[0],
                    MACH * gx[2] + gy[0],
                    MACH * gx[3] + gz[0],
                ]
                for f in range(4):
                    rate[f] = rate[f] + size_y * dy[f][g] + size_z * dz[f][g]
                rate[0] = rate[0] + sign_y * dy[2][g] + sign_z * dz[3][g]
                rate[2] = rate[2] + sign_y * dy[0][g]
                rate[3] = rate[3] + sign_z * dz[0][g]
                if t in (0, 3):
                    s = -1.0 if t == 0 else 1.0
                    d = [dx[f][g] for f in range(4)]
                    own = -HALF_LIFT * (s * MACH + ALPHA)
                    rate[0] = rate[0] + own * d[0] - (HALF_LIFT * s) * d[1]
                    rate[1] = rate[1] + own * d[1] - (HALF_LIFT * s) * d[0]
                    rate[2] = rate[2] + own * d[2]
                    rate[3] = rate[3] + own * d[3]
                new = [q[f][g] + TIME_STEP * rate[f] for f in range(4)]
                source = ground[pl.ds(pl.multiple_of(a * 16 + 8 * g, 8), 8), here]
                new[0] = new[0] + (TIME_STEP * SOURCE_GAIN) * source
                for f in range(4):
                    out_ref[f, a, 8 * g : 8 * g + 8, here] = new[f]
        return carry

    lax.fori_loop(0, 8, step, 0)


def finish_kernel(
    arrival_ref, adj_ref, new_ref, before_along, after_along, before_cross, after_cross, received_ref,
    next_ref, kappa_ref, edge,
):
    lift = TIME_STEP * HALF_LIFT
    lane = lanes((4, 128))
    j = (lane >> 3) & 7

    def along_terms(ref, s, rows):
        q = [pltpu.roll(ref[f, rows, :], 64, 1) for f in range(4)]
        own = lift * (s * MACH + ALPHA)
        return [own * q[0] + (lift * s) * q[1], own * q[1] + (lift * s) * q[0], own * q[2], own * q[3]]

    def cross_terms(ref, s, t):
        q = [ref[f, :, tile(t)] for f in range(4)]
        own = lift * ALPHA
        return [
            own * q[0] + (lift * s) * q[2], own * q[1], own * q[2] + (lift * s) * q[0], own * q[3],
        ]

    for c in range(4):
        rows = slice(4 * c, 4 * c + 4)
        low = along_terms(before_along, -1.0, rows)
        high = along_terms(after_along, 1.0, rows)
        for f in range(4):
            edge[0, f, rows, :] = jnp.where(lane < 64, low[f], 0.0)
            edge[1, f, rows, :] = jnp.where(lane >= 64, high[f], 0.0)
    for t in range(4):
        low = cross_terms(before_cross, -1.0, t)
        high = cross_terms(after_cross, 1.0, t)
        for a in range(8):
            for f in range(4):
                for c in range(4):
                    value = new_ref[f, a, 4 * c : 4 * c + 4, tile(t)]
                    if c == 0:
                        value = value + jnp.where(j == 0, pltpu.roll(low[f], (128 - 8 * a) % 128, 1), 0.0)
                    if c == 3:
                        value = value + jnp.where(j == 7, pltpu.roll(high[f], (56 - 8 * a) % 128, 1), 0.0)
                    if t == 0 and a == 0:
                        value = value + edge[0, f, 4 * c : 4 * c + 4, :]
                    if t == 3 and a == 7:
                        value = value + edge[1, f, 4 * c : 4 * c + 4, :]
                    next_ref[f, a, c, :, tile(t)] = value
    for a in range(8):
        for c in range(4):
            q = arrival_ref[a, c]
            clipped = jnp.maximum(q, 0)
            holder = clipped >> 1
            second = (clipped & 1) == 1
            block = jnp.where(second, received_ref[holder, 4:8, :], received_ref[holder, 0:4, :])
            value = TIME_STEP * adj_ref[0, a, c] * block
            kappa_ref[a, c] = jnp.where(q >= 0, value, 0.0)


VMEM = pl.BlockSpec(memory_space=pltpu.VMEM)
SMEM = pl.BlockSpec(memory_space=pltpu.SMEM)


def kernel(body, out_shape, in_specs, scratch, flops, moved):
    return pl.pallas_call(
        body,
        out_shape=out_shape,
        in_specs=in_specs,
        out_specs=jax.tree.map(lambda _: VMEM, out_shape),
        scratch_shapes=scratch,
        compiler_params=pltpu.CompilerParams(vmem_limit_bytes=VMEM_BYTES),
        cost_estimate=pl.CostEstimate(flops=flops, bytes_accessed=moved, transcendentals=0),
    )


def array(*shape):
    return jax.ShapeDtypeStruct(shape, F32)


def shift(value, axis, up):
    peers = lax.axis_size(axis)
    pairs = [(i, i + 1) for i in range(peers - 1)]
    if not up:
        pairs = [(j, i) for i, j in pairs]
    return lax.ppermute(value, axis, pairs)


def per_device(adjoint_state, snapshot_store, dispatch_slot, arrival_slot, mic_node, mic_residual):
    gx, gyz = (jnp.asarray(table) for table in derivative_tables())
    outgoing, last_along, first_along, last_cross, first_cross = kernel(
        holder_kernel,
        (array(32, 8, 512), array(4, 16, 128), array(4, 16, 128), array(4, 4, 512), array(4, 4, 512)),
        [SMEM, VMEM, VMEM, VMEM, VMEM],
        [
            pltpu.VMEM((3, 16, 16, 512), F32),
            pltpu.VMEM((3, 256, 512), BF16),
            pltpu.VMEM((3, 256, 512), BF16),
        ],
        3_000_000_000, 5_000_000,
    )(dispatch_slot, adjoint_state, snapshot_store, gx, gyz)
    received = lax.all_to_all(outgoing, "cross", split_axis=0, concat_axis=0, tiled=True)
    before_along = shift(last_along, "along", True)
    after_along = shift(first_along, "along", False)
    before_cross = shift(last_cross, "cross", True)
    after_cross = shift(first_cross, "cross", False)
    updated = kernel(
        volume_kernel,
        array(4, 8, 16, 512),
        [VMEM] * 5,
        [
            pltpu.VMEM((4, 10, 16, 512), F32),
            pltpu.VMEM((512, 512), BF16),
            pltpu.VMEM((512, 512), BF16),
            pltpu.VMEM((512, 512), F32),
            pltpu.VMEM((256, 512), F32),
            pltpu.VMEM((256, 512), F32),
            pltpu.VMEM((128, 512), F32),
        ],
        4_000_000_000, 4_000_000,
    )(mic_node.reshape(1, 128), mic_residual.reshape(1, 128), adjoint_state, gx, gyz)
    return kernel(
        finish_kernel,
        (array(4, 8, 4, 4, 512), array(8, 4, 4, 512)),
        [SMEM] + [VMEM] * 7,
        [pltpu.VMEM((2, 4, 16, 128), F32)],
        10_000_000, 4_000_000,
    )(
        arrival_slot, adjoint_state, updated, before_along, after_along, before_cross, after_cross, received
    )


def solution(mesh):
    in_specs = (
        P(None, "along", "cross", None, None),
        P(("along", "cross"), None, None, None),
        P(("along", "cross")),
        P("along", "cross"),
        P(("along", "cross")),
        P(("along", "cross")),
    )
    out_specs = (P(None, "along", "cross", None, None), P("along", "cross", None, None))
    return jax.shard_map(
        per_device, mesh=mesh, in_specs=in_specs, out_specs=out_specs, check_vma=False
    )
```

```python
import jax
import jax.numpy as jnp
import numpy as np
from jax import lax
from jax.experimental import pallas as pl
from jax.experimental.pallas import tpu as pltpu
from jax.sharding import PartitionSpec as P

MACH = 0.3
ALPHA = 1.3
LIFT_SCALE = 56.0
TIME_STEP = 0.004
SOURCE_GAIN = 50.0
HALF_LIFT = 0.5 * LIFT_SCALE
LOBATTO_INNER = [
    -0.8717401485096066,
    -0.5917001814331423,
    -0.2092992179024789,
    0.2092992179024789,
    0.5917001814331423,
    0.8717401485096066,
]
F32 = jnp.float32
BF16 = jnp.bfloat16
VMEM_BYTES = 24 * 1024 * 1024
HOLDER_BYTES = 60_000_000


def legendre_seven(points):
    previous = points * 0.0 + 1.0
    current = points * 1.0
    for degree_index in range(1, 7):
        following = ((2 * degree_index + 1) * points * current - degree_index * previous) / (
            degree_index + 1
        )
        previous, current = (current, following)
    return current


def derivative_rows():
    degree = 7
    points = np.array([-1.0] + LOBATTO_INNER + [1.0])
    values = legendre_seven(points)
    differ = points[:, None] - points[None, :] + np.eye(degree + 1)
    matrix = values[:, None] / values[None, :] / differ
    matrix = matrix * (1.0 - np.eye(degree + 1))
    matrix[0, 0] = -degree * (degree + 1) / 4.0
    matrix[degree, degree] = degree * (degree + 1) / 4.0
    twice = 2.0 * matrix.T
    rows = np.stack(
        [np.repeat(twice, 64, axis=1), np.tile(np.repeat(twice, 8, axis=1), 8), np.tile(twice, 64)]
    ).astype(np.float32)
    high = rows.astype(BF16)
    low = (rows - high.astype(np.float32)).astype(BF16)
    return np.stack([high, low]).astype(np.float32)


def fill_table(rows_ref, table):
    lane = lanes((16, 128))
    sub = lax.broadcasted_iota(jnp.int32, (16, 128), 0)
    upper = sub >= 8
    zero = jnp.zeros((16, 128), F32)
    for h in range(2):
        for i in range(8):
            for t in range(4):
                row = rows_ref[h, 0, i : i + 1, tile(t)]
                for m in range(4):
                    value = jnp.where((lane & 63) == sub + 16 * m, row, zero)
                    table[h, 64 * i + 16 * m : 64 * i + 16 * m + 16, tile(t)] = value.astype(BF16)
        row = rows_ref[h, 2, :, tile(0)]
        vertical = jnp.concatenate([row, row], axis=0)
        for g in range(16):
            here = g // 8
            j = 2 * g % 8
            row = jnp.where(upper, rows_ref[h, 1, j + 1 : j + 2, tile(0)], rows_ref[h, 1, j : j + 1, tile(0)])
            inside = ((lane >> 6) == g // 4 % 2) & ((lane & 7) == (sub & 7))
            cross = jnp.where(inside, row, zero).astype(BF16)
            inside = (lane >> 3) == (sub >> 3) + 2 * (g % 8)
            level = jnp.where(inside, vertical, zero).astype(BF16)
            for t in range(2):
                table[h, 16 * g : 16 * g + 16, tile(4 + t)] = cross if t == here else zero.astype(BF16)
                table[h, 256 + 16 * g : 272 + 16 * g, tile(4 + t)] = level if t == here else zero.astype(BF16)


def split(x):
    high = x.astype(BF16)
    return high, (x - high.astype(F32)).astype(BF16)


def product(high, low, table_high, table_low):
    def dot(a, b):
        return jnp.dot(a, b, preferred_element_type=F32)

    return dot(high, table_high) + (dot(low, table_high) + dot(high, table_low))


def lanes(shape):
    return lax.broadcasted_iota(jnp.int32, shape, len(shape) - 1)


def tile(t):
    return slice(128 * t, 128 * t + 128)


def is_even(axis):
    return (lax.axis_index(axis) & 1) == 0


def holder_kernel(
    slot_hbm, adj_hbm, store_hbm, rows_hbm,
    out_hbm, along_one, along_two, cross_one, cross_two,
    slot_ref, store_ref, rows_ref, table, face_along, face_cross, stage, high, low, total, sems,
):
    pieces = [
        (slot_hbm, slot_ref),
        (store_hbm, store_ref),
        (adj_hbm.at[:, 0, :, :, tile(0)], face_along.at[0]),
        (adj_hbm.at[:, 7, :, :, tile(3)], face_along.at[1]),
        (adj_hbm.at[:, :, 0], face_cross.at[0]),
        (adj_hbm.at[:, :, 3], face_cross.at[1]),
        (rows_hbm, rows_ref),
    ]
    copies = [pltpu.make_async_copy(src, dst, sems.at[n]) for n, (src, dst) in enumerate(pieces)]
    for copy in copies:
        copy.start()
    for n in (2, 3, 4, 5):
        copies[n].wait()
    even = is_even("along")
    for f in range(4):
        for c in range(4):
            rows = slice(4 * c, 4 * c + 4)
            first = face_along[0, f, c]
            last = face_along[1, f, c]
            along_one[f, rows, :] = jnp.where(even, last, first)
            along_two[f, rows, :] = jnp.where(even, first, last)
    even = is_even("cross")
    j = (lanes((4, 128)) >> 3) & 7
    for f in range(4):
        for t in range(4):
            last = pltpu.roll(face_cross[1, f, 0, :, tile(t)], 72, 1)
            first = face_cross[0, f, 0, :, tile(t)]
            for a in range(1, 8):
                other = face_cross[1, f, a, :, tile(t)]
                last = jnp.where(j == a, pltpu.roll(other, (72 + 8 * a) % 128, 1), last)
                other = face_cross[0, f, a, :, tile(t)]
                first = jnp.where(j == a, pltpu.roll(other, 8 * a, 1), first)
            cross_one[f, :, tile(t)] = jnp.where(even, last, first)
            cross_two[f, :, tile(t)] = jnp.where(even, first, last)
    copies[6].wait()
    fill_table(rows_ref, table)
    copies[0].wait()
    copies[1].wait()

    def gather(g, carry):
        rows = pl.ds(pl.multiple_of(g * 16, 16), 16)
        for m in range(4):
            slot = slot_ref[4 * g + m]
            for f in range(3):
                stage[f, g, 4 * m : 4 * m + 4, :] = store_ref[slot, f]
        for f in range(3):
            high[f, rows], low[f, rows] = split(stage[f, g])
        return carry

    lax.fori_loop(0, 16, gather, 0)
    writes = []
    for c in range(2):
        part = slice(256 * c, 256 * c + 256)
        spread = product(high[0], low[0], table[0, :, part], table[1, :, part])
        for f in (1, 2):
            rows = slice(256 * (f - 1), 256 * f)
            spread += product(high[f, :, part], low[f, :, part], table[0, rows, 512:768], table[1, rows, 512:768])
        total[:, :, part] = spread.reshape(32, 8, 256)
        writes.append(
            pltpu.make_async_copy(total.at[:, :, part], out_hbm.at[:, :, part], sems.at[7 + c])
        )
        writes[c].start()
    for write in writes:
        write.wait()


def volume_kernel(
    node_ref, residual_ref, adj_ref, rows_ref, out_ref, table, state, high, low, slope_x, slope_y, slope_z, ground
):
    fill_table(rows_ref, table)
    order = (2, 0, 3, 1)
    row = {f: 128 * n for n, f in enumerate(order)}
    state[:, 0] = jnp.zeros((4, 16, 512), F32)
    state[:, 9] = jnp.zeros((4, 16, 512), F32)

    def load(a, carry):
        for f in range(4):
            for c in range(4):
                state[f, a + 1, 4 * c : 4 * c + 4, :] = adj_ref[f, a, c]
            rows = pl.ds(pl.multiple_of(row[f] + a * 16, 16), 16)
            high[rows], low[rows] = split(state[f, a + 1])
        return carry

    lax.fori_loop(0, 8, load, 0)
    for c in range(2):
        part = slice(256 * c, 256 * c + 256)
        slope_x[:, part] = product(high[...], low[...], table[0, :, part], table[1, :, part])
        slope_y[:, part] = product(
            high[0:256, part], low[0:256, part], table[0, 0:256, 512:768], table[1, 0:256, 512:768]
        )
        slope_z[:, part] = product(
            high[128:384, part], low[128:384, part], table[0, 256:512, 512:768], table[1, 256:512, 512:768]
        )

    node = node_ref[...]
    residual = residual_ref[...]
    target = lax.broadcasted_iota(jnp.int32, (128, 128), 0)
    spread = jnp.where(target == 4 * (node >> 6), residual, 0.0)
    place = lax.broadcasted_iota(jnp.int32, (512, 128), 0) == 8 * (node & 63)
    place = jnp.where(place, 1.0, 0.0).astype(BF16)
    ones, rest = split(spread)
    twos = (spread - ones.astype(F32) - rest.astype(F32)).astype(BF16)

    def match(a):
        return lax.dot_general(a, place, (((1,), (1,)), ((), ())), preferred_element_type=F32)

    ground[...] = match(ones) + (match(rest) + match(twos))

    lane = lanes((8, 128))
    sub = lax.broadcasted_iota(jnp.int32, (8, 128), 0)
    j = (lane >> 3) & 7
    k = lane & 7
    e = sub & 3
    odd = sub >= 4
    top_y = j == 7
    top_z = k == 7
    floor = e == 0
    ceiling = e == 3
    zero = jnp.zeros((8, 128), F32)
    sign_y = jnp.where(j == 0, HALF_LIFT, jnp.where(top_y, -HALF_LIFT, 0.0))
    size_y = jnp.where((j == 0) | top_y, -HALF_LIFT * ALPHA, 0.0)
    sign_z = jnp.where(k == 0, HALF_LIFT, jnp.where(top_z, -HALF_LIFT, 0.0))
    size_z = jnp.where((k == 0) | top_z, -HALF_LIFT * ALPHA, 0.0)

    def step(a, carry):
        for t in range(4):
            here = tile(t)
            q = [[state[f, a + 1, 8 * g : 8 * g + 8, here] for g in range(2)] for f in range(4)]
            dy = [[None] * 2 for _ in range(4)]
            dz = [[None] * 2 for _ in range(4)]
            dx = [[None] * 2 for _ in range(4)]
            for f in range(4):
                swap = [pltpu.roll(q[f][g], 4, 0) for g in range(2)]
                before = [jnp.where(odd, swap[0], zero), jnp.where(odd, swap[1], swap[0])]
                after = [jnp.where(odd, swap[1], swap[0]), jnp.where(odd, zero, swap[1])]
                for g in range(2):
                    x = q[f][g]
                    outer = jnp.where(top_y, pltpu.roll(after[g], 56, 1), pltpu.roll(before[g], 72, 1))
                    dy[f][g] = x - outer
                    below = pltpu.roll(pltpu.roll(x, 1, 0), 121, 1)
                    below = jnp.where(floor, -x if f == 3 else x, below)
                    above = pltpu.roll(pltpu.roll(x, 7, 0), 7, 1)
                    above = jnp.where(ceiling, zero, above)
                    dz[f][g] = x - jnp.where(top_z, above, below)
                    if t == 0:
                        outer = pltpu.roll(state[f, a, 8 * g : 8 * g + 8, tile(3)], 64, 1)
                        dx[f][g] = jnp.where(lane < 64, x - outer, zero)
                    if t == 3:
                        outer = pltpu.roll(state[f, a + 2, 8 * g : 8 * g + 8, tile(0)], 64, 1)
                        dx[f][g] = jnp.where(lane >= 64, x - outer, zero)
            for g in range(2):
                def rows(f, base=0):
                    return pl.ds(pl.multiple_of(row[f] - base + a * 16 + 8 * g, 8), 8)

                gx = [slope_x[rows(f), here] for f in range(4)]
                gy = {f: slope_y[rows(f), here] for f in (2, 0)}
                gz = {f: slope_z[rows(f, 128), here] for f in (0, 3)}
                rate = [
                    MACH * gx[0] + gx[1] + gy[2] + gz[3],
                    MACH * gx[1] + gx[0],
                    MACH * gx[2] + gy[0],
                    MACH * gx[3] + gz[0],
                ]
                for f in range(4):
                    rate[f] = rate[f] + size_y * dy[f][g] + size_z * dz[f][g]
                rate[0] = rate[0] + sign_y * dy[2][g] + sign_z * dz[3][g]
                rate[2] = rate[2] + sign_y * dy[0][g]
                rate[3] = rate[3] + sign_z * dz[0][g]
                if t in (0, 3):
                    s = -1.0 if t == 0 else 1.0
                    d = [dx[f][g] for f in range(4)]
                    own = -HALF_LIFT * (s * MACH + ALPHA)
                    rate[0] = rate[0] + own * d[0] - (HALF_LIFT * s) * d[1]
                    rate[1] = rate[1] + own * d[1] - (HALF_LIFT * s) * d[0]
                    rate[2] = rate[2] + own * d[2]
                    rate[3] = rate[3] + own * d[3]
                new = [q[f][g] + TIME_STEP * rate[f] for f in range(4)]
                source = ground[pl.ds(pl.multiple_of(a * 16 + 8 * g, 8), 8), here]
                new[0] = new[0] + (TIME_STEP * SOURCE_GAIN) * source
                for f in range(4):
                    out_ref[f, a, 8 * g : 8 * g + 8, here] = new[f]
        return carry

    lax.fori_loop(0, 8, step, 0)


def finish_kernel(
    arrival_ref, adj_ref, new_ref, along_one, along_two, cross_one, cross_two, received_ref,
    next_ref, kappa_ref, edge,
):
    lift = TIME_STEP * HALF_LIFT
    lane = lanes((4, 128))
    j = (lane >> 3) & 7

    def arrived(axis, one, two, s, f, index):
        use_one = is_even(axis) if s > 0 else jnp.logical_not(is_even(axis))
        return jnp.where(use_one, one[(f, *index)], two[(f, *index)])

    def along_terms(s, rows):
        q = [arrived("along", along_one, along_two, s, f, (rows, slice(None))) for f in range(4)]
        q = [pltpu.roll(x, 64, 1) for x in q]
        own = lift * (s * MACH + ALPHA)
        return [own * q[0] + (lift * s) * q[1], own * q[1] + (lift * s) * q[0], own * q[2], own * q[3]]

    def cross_terms(s, t):
        q = [arrived("cross", cross_one, cross_two, s, f, (slice(None), tile(t))) for f in range(4)]
        own = lift * ALPHA
        return [
            own * q[0] + (lift * s) * q[2], own * q[1], own * q[2] + (lift * s) * q[0], own * q[3],
        ]

    for c in range(4):
        rows = slice(4 * c, 4 * c + 4)
        low = along_terms(-1.0, rows)
        high = along_terms(1.0, rows)
        for f in range(4):
            edge[0, f, rows, :] = jnp.where(lane < 64, low[f], 0.0)
            edge[1, f, rows, :] = jnp.where(lane >= 64, high[f], 0.0)
    for t in range(4):
        low = cross_terms(-1.0, t)
        high = cross_terms(1.0, t)
        for a in range(8):
            for f in range(4):
                for c in range(4):
                    value = new_ref[f, a, 4 * c : 4 * c + 4, tile(t)]
                    if c == 0:
                        value = value + jnp.where(j == 0, pltpu.roll(low[f], (128 - 8 * a) % 128, 1), 0.0)
                    if c == 3:
                        value = value + jnp.where(j == 7, pltpu.roll(high[f], (56 - 8 * a) % 128, 1), 0.0)
                    if t == 0 and a == 0:
                        value = value + edge[0, f, 4 * c : 4 * c + 4, :]
                    if t == 3 and a == 7:
                        value = value + edge[1, f, 4 * c : 4 * c + 4, :]
                    next_ref[f, a, c, :, tile(t)] = value
    for a in range(8):
        for c in range(4):
            q = arrival_ref[a, c]
            clipped = jnp.maximum(q, 0)
            holder = clipped >> 1
            second = (clipped & 1) == 1
            block = jnp.where(second, received_ref[holder, 4:8, :], received_ref[holder, 0:4, :])
            value = TIME_STEP * adj_ref[0, a, c] * block
            kappa_ref[a, c] = jnp.where(q >= 0, value, 0.0)


VMEM = pl.BlockSpec(memory_space=pltpu.VMEM)
HBM = pl.BlockSpec(memory_space=pltpu.HBM)
SMEM = pl.BlockSpec(memory_space=pltpu.SMEM)


def kernel(body, out_shape, in_specs, scratch, flops, moved, out_specs=None, limit=VMEM_BYTES):
    return pl.pallas_call(
        body,
        out_shape=out_shape,
        in_specs=in_specs,
        out_specs=out_specs or jax.tree.map(lambda _: VMEM, out_shape),
        scratch_shapes=scratch,
        compiler_params=pltpu.CompilerParams(vmem_limit_bytes=limit),
        cost_estimate=pl.CostEstimate(flops=flops, bytes_accessed=moved, transcendentals=0),
    )


def array(*shape):
    return jax.ShapeDtypeStruct(shape, F32)


def exchange(value, axis, start):
    pairs = []
    for i in range(start, lax.axis_size(axis) - 1, 2):
        pairs += [(i, i + 1), (i + 1, i)]
    return lax.ppermute(value, axis, pairs)


def per_device(adjoint_state, snapshot_store, dispatch_slot, arrival_slot, mic_node, mic_residual):
    rows = jnp.asarray(derivative_rows())
    outgoing, along_one, along_two, cross_one, cross_two = kernel(
        holder_kernel,
        (array(32, 8, 512), array(4, 16, 128), array(4, 16, 128), array(4, 4, 512), array(4, 4, 512)),
        [HBM] * 4,
        [
            pltpu.SMEM((64,), jnp.int32),
            pltpu.VMEM((64, 3, 4, 512), F32),
            pltpu.VMEM((2, 3, 8, 512), F32),
            pltpu.VMEM((2, 512, 768), BF16),
            pltpu.VMEM((2, 4, 4, 4, 128), F32),
            pltpu.VMEM((2, 4, 8, 4, 512), F32),
            pltpu.VMEM((3, 16, 16, 512), F32),
            pltpu.VMEM((3, 256, 512), BF16),
            pltpu.VMEM((3, 256, 512), BF16),
            pltpu.VMEM((32, 8, 512), F32),
            pltpu.SemaphoreType.DMA((9,)),
        ],
        3_000_000_000, 5_000_000,
        (HBM, VMEM, VMEM, VMEM, VMEM),
        HOLDER_BYTES,
    )(dispatch_slot, adjoint_state, snapshot_store, rows)
    received = lax.all_to_all(outgoing, "cross", split_axis=0, concat_axis=0, tiled=True)
    along_one = exchange(along_one, "along", 0)
    along_two = exchange(along_two, "along", 1)
    cross_one = exchange(cross_one, "cross", 0)
    cross_two = exchange(cross_two, "cross", 1)
    updated = kernel(
        volume_kernel,
        array(4, 8, 16, 512),
        [VMEM] * 4,
        [
            pltpu.VMEM((2, 512, 768), BF16),
            pltpu.VMEM((4, 10, 16, 512), F32),
            pltpu.VMEM((512, 512), BF16),
            pltpu.VMEM((512, 512), BF16),
            pltpu.VMEM((512, 512), F32),
            pltpu.VMEM((256, 512), F32),
            pltpu.VMEM((256, 512), F32),
            pltpu.VMEM((128, 512), F32),
        ],
        4_000_000_000, 4_000_000,
    )(mic_node.reshape(1, 128), mic_residual.reshape(1, 128), adjoint_state, rows)
    return kernel(
        finish_kernel,
        (array(4, 8, 4, 4, 512), array(8, 4, 4, 512)),
        [SMEM] + [VMEM] * 7,
        [pltpu.VMEM((2, 4, 16, 128), F32)],
        10_000_000, 4_000_000,
    )(
        arrival_slot, adjoint_state, updated, along_one, along_two, cross_one, cross_two, received
    )


def solution(mesh):
    in_specs = (
        P(None, "along", "cross", None, None),
        P(("along", "cross"), None, None, None),
        P(("along", "cross")),
        P("along", "cross"),
        P(("along", "cross")),
        P(("along", "cross")),
    )
    out_specs = (P(None, "along", "cross", None, None), P("along", "cross", None, None))
    return jax.shard_map(
        per_device, mesh=mesh, in_specs=in_specs, out_specs=out_specs, check_vma=False
    )
```

```python
import jax
import jax.numpy as jnp
import numpy as np
from jax import lax
from jax.experimental import pallas as pl
from jax.experimental.pallas import tpu as pltpu
from jax.sharding import PartitionSpec as P

MACH = 0.3
ALPHA = 1.3
LIFT_SCALE = 56.0
TIME_STEP = 0.004
SOURCE_GAIN = 50.0
HALF_LIFT = 0.5 * LIFT_SCALE
LOBATTO_INNER = [
    -0.8717401485096066,
    -0.5917001814331423,
    -0.2092992179024789,
    0.2092992179024789,
    0.5917001814331423,
    0.8717401485096066,
]
F32 = jnp.float32
BF16 = jnp.bfloat16
VMEM_BYTES = 24 * 1024 * 1024
HOLDER_BYTES = 60_000_000


def legendre_seven(points):
    previous = points * 0.0 + 1.0
    current = points * 1.0
    for degree_index in range(1, 7):
        following = ((2 * degree_index + 1) * points * current - degree_index * previous) / (
            degree_index + 1
        )
        previous, current = (current, following)
    return current


def derivative_rows():
    degree = 7
    points = np.array([-1.0] + LOBATTO_INNER + [1.0])
    values = legendre_seven(points)
    differ = points[:, None] - points[None, :] + np.eye(degree + 1)
    matrix = values[:, None] / values[None, :] / differ
    matrix = matrix * (1.0 - np.eye(degree + 1))
    matrix[0, 0] = -degree * (degree + 1) / 4.0
    matrix[degree, degree] = degree * (degree + 1) / 4.0
    twice = 2.0 * matrix
    half = np.arange(128) // 64
    along = np.zeros((4, 4, 2, 128))
    for t in range(4):
        for source in range(4):
            along[t, source, 0] = twice[2 * t + half, 2 * source + half]
            along[t, source, 1] = twice[2 * t + half, 2 * source + 1 - half]
    rows = np.stack([np.tile(np.repeat(twice.T, 8, axis=1), 2), np.tile(twice.T, 16)]).astype(np.float32)
    high = rows.astype(BF16)
    low = (rows - high.astype(np.float32)).astype(BF16)
    parts = [along.reshape(32, 128), *high, *low]
    return np.concatenate([part.astype(np.float32) for part in parts])


def along_slope(x, rows_ref):
    turned = [pltpu.roll(value, 64, 1) for value in x]
    slopes = []
    for t in range(4):
        slope = None
        for s in range(4):
            n = 8 * t + 2 * s
            term = rows_ref[n : n + 1, :] * x[s] + rows_ref[n + 1 : n + 2, :] * turned[s]
            slope = term if slope is None else slope + term
        slopes.append(slope)
    return slopes


def fill_table(rows_ref, table):
    lane = lanes((16, 128))
    sub = lax.broadcasted_iota(jnp.int32, (16, 128), 0)
    zero = jnp.zeros((16, 128), F32)
    table[...] = jnp.zeros((2, 512, 256), BF16)
    for h in range(2):
        base = 32 + 16 * h
        row = rows_ref[base + 8 : base + 16, :]
        vertical = jnp.concatenate([row, row], axis=0)
        for g in range(16):
            here = tile(g // 8)
            j = base + 2 * g % 8
            row = jnp.where(sub >= 8, rows_ref[j + 1 : j + 2, :], rows_ref[j : j + 1, :])
            inside = ((lane >> 6) == g // 4 % 2) & ((lane & 7) == (sub & 7))
            table[h, 16 * g : 16 * g + 16, here] = jnp.where(inside, row, zero).astype(BF16)
            inside = (lane >> 3) == (sub >> 3) + 2 * (g % 8)
            table[h, 256 + 16 * g : 272 + 16 * g, here] = jnp.where(inside, vertical, zero).astype(BF16)


def split(x):
    high = x.astype(BF16)
    return high, (x - high.astype(F32)).astype(BF16)


def product(high, low, table_high, table_low):
    def dot(a, b):
        return jnp.dot(a, b, preferred_element_type=F32)

    return dot(high, table_high) + (dot(low, table_high) + dot(high, table_low))


def lanes(shape):
    return lax.broadcasted_iota(jnp.int32, shape, len(shape) - 1)


def tile(t):
    return slice(128 * t, 128 * t + 128)


def is_even(axis):
    return (lax.axis_index(axis) & 1) == 0


def holder_kernel(
    slot_hbm, adj_hbm, store_hbm, rows_hbm,
    out_hbm, along_one, along_two, cross_one, cross_two,
    slot_ref, store_ref, rows_ref, table, face_along, face_cross, stage, high, low, total, sems,
):
    pieces = [
        (slot_hbm, slot_ref),
        (store_hbm, store_ref),
        (adj_hbm.at[:, 0, :, :, tile(0)], face_along.at[0]),
        (adj_hbm.at[:, 7, :, :, tile(3)], face_along.at[1]),
        (adj_hbm.at[:, :, 0], face_cross.at[0]),
        (adj_hbm.at[:, :, 3], face_cross.at[1]),
        (rows_hbm, rows_ref),
    ]
    copies = [pltpu.make_async_copy(src, dst, sems.at[n]) for n, (src, dst) in enumerate(pieces)]
    for copy in copies:
        copy.start()
    for n in (2, 3, 4, 5):
        copies[n].wait()
    even = is_even("along")
    for f in range(4):
        for c in range(4):
            rows = slice(4 * c, 4 * c + 4)
            first = face_along[0, f, c]
            last = face_along[1, f, c]
            along_one[f, rows, :] = jnp.where(even, last, first)
            along_two[f, rows, :] = jnp.where(even, first, last)
    even = is_even("cross")
    j = (lanes((4, 128)) >> 3) & 7
    for f in range(4):
        for t in range(4):
            last = pltpu.roll(face_cross[1, f, 0, :, tile(t)], 72, 1)
            first = face_cross[0, f, 0, :, tile(t)]
            for a in range(1, 8):
                other = face_cross[1, f, a, :, tile(t)]
                last = jnp.where(j == a, pltpu.roll(other, (72 + 8 * a) % 128, 1), last)
                other = face_cross[0, f, a, :, tile(t)]
                first = jnp.where(j == a, pltpu.roll(other, 8 * a, 1), first)
            cross_one[f, :, tile(t)] = jnp.where(even, last, first)
            cross_two[f, :, tile(t)] = jnp.where(even, first, last)
    copies[6].wait()
    fill_table(rows_ref, table)
    copies[0].wait()
    copies[1].wait()

    def gather(g, carry):
        rows = pl.ds(pl.multiple_of(g * 16, 16), 16)
        for m in range(4):
            slot = slot_ref[4 * g + m]
            for f in range(3):
                stage[f, g, 4 * m : 4 * m + 4, :] = store_ref[slot, f]
        slopes = along_slope([stage[0, g, :, tile(t)] for t in range(4)], rows_ref)
        for t in range(4):
            total[pl.ds(2 * g, 2), :, tile(t)] = slopes[t].reshape(2, 8, 128)
        for f in range(2):
            high[f, rows], low[f, rows] = split(stage[f + 1, g])
        return carry

    lax.fori_loop(0, 16, gather, 0, unroll=16)
    writes = []
    for c in range(2):
        part = slice(256 * c, 256 * c + 256)
        spread = product(high[0, :, part], low[0, :, part], table[0, 0:256], table[1, 0:256])
        spread += product(high[1, :, part], low[1, :, part], table[0, 256:512], table[1, 256:512])
        total[:, :, part] += spread.reshape(32, 8, 256)
        writes.append(
            pltpu.make_async_copy(total.at[:, :, part], out_hbm.at[:, :, part], sems.at[7 + c])
        )
        writes[c].start()
    for write in writes:
        write.wait()


def volume_kernel(
    node_ref, residual_ref, adj_ref, rows_ref, out_ref, table, state, high, low, slope_x, slope_y, slope_z, ground
):
    fill_table(rows_ref, table)
    row = {2: 0, 0: 128, 3: 256}
    state[:, 0] = jnp.zeros((4, 16, 512), F32)
    state[:, 9] = jnp.zeros((4, 16, 512), F32)

    def load(a, carry):
        for f in range(4):
            for c in range(4):
                state[f, a + 1, 4 * c : 4 * c + 4, :] = adj_ref[f, a, c]
            slopes = along_slope([state[f, a + 1, :, tile(t)] for t in range(4)], rows_ref)
            for t in range(4):
                slope_x[f, a, :, tile(t)] = slopes[t]
            if f in row:
                rows = pl.ds(pl.multiple_of(row[f] + a * 16, 16), 16)
                high[rows], low[rows] = split(state[f, a + 1])
        return carry

    lax.fori_loop(0, 8, load, 0, unroll=8)
    for c in range(2):
        part = slice(256 * c, 256 * c + 256)
        slope_y[:, part] = product(high[0:256, part], low[0:256, part], table[0, 0:256], table[1, 0:256])
        slope_z[:, part] = product(
            high[128:384, part], low[128:384, part], table[0, 256:512], table[1, 256:512]
        )

    node = node_ref[...]
    residual = residual_ref[...]
    target = lax.broadcasted_iota(jnp.int32, (128, 128), 0)
    spread = jnp.where(target == 4 * (node >> 6), residual, 0.0)
    place = lax.broadcasted_iota(jnp.int32, (512, 128), 0) == 8 * (node & 63)
    place = jnp.where(place, 1.0, 0.0).astype(BF16)
    ones, rest = split(spread)
    twos = (spread - ones.astype(F32) - rest.astype(F32)).astype(BF16)

    def match(a):
        return lax.dot_general(a, place, (((1,), (1,)), ((), ())), preferred_element_type=F32)

    ground[...] = match(ones) + (match(rest) + match(twos))

    lane = lanes((8, 128))
    sub = lax.broadcasted_iota(jnp.int32, (8, 128), 0)
    j = (lane >> 3) & 7
    k = lane & 7
    e = sub & 3
    odd = sub >= 4
    top_y = j == 7
    top_z = k == 7
    floor = e == 0
    ceiling = e == 3
    zero = jnp.zeros((8, 128), F32)
    sign_y = jnp.where(j == 0, HALF_LIFT, jnp.where(top_y, -HALF_LIFT, 0.0))
    size_y = jnp.where((j == 0) | top_y, -HALF_LIFT * ALPHA, 0.0)
    sign_z = jnp.where(k == 0, HALF_LIFT, jnp.where(top_z, -HALF_LIFT, 0.0))
    size_z = jnp.where((k == 0) | top_z, -HALF_LIFT * ALPHA, 0.0)

    def step(a, carry):
        for t in range(4):
            here = tile(t)
            q = [[state[f, a + 1, 8 * g : 8 * g + 8, here] for g in range(2)] for f in range(4)]
            dy = [[None] * 2 for _ in range(4)]
            dz = [[None] * 2 for _ in range(4)]
            dx = [[None] * 2 for _ in range(4)]
            for f in range(4):
                swap = [pltpu.roll(q[f][g], 4, 0) for g in range(2)]
                before = [jnp.where(odd, swap[0], zero), jnp.where(odd, swap[1], swap[0])]
                after = [jnp.where(odd, swap[1], swap[0]), jnp.where(odd, zero, swap[1])]
                for g in range(2):
                    x = q[f][g]
                    outer = jnp.where(top_y, pltpu.roll(after[g], 56, 1), pltpu.roll(before[g], 72, 1))
                    dy[f][g] = x - outer
                    below = pltpu.roll(pltpu.roll(x, 1, 0), 121, 1)
                    below = jnp.where(floor, -x if f == 3 else x, below)
                    above = pltpu.roll(pltpu.roll(x, 7, 0), 7, 1)
                    above = jnp.where(ceiling, zero, above)
                    dz[f][g] = x - jnp.where(top_z, above, below)
                    if t == 0:
                        outer = pltpu.roll(state[f, a, 8 * g : 8 * g + 8, tile(3)], 64, 1)
                        dx[f][g] = jnp.where(lane < 64, x - outer, zero)
                    if t == 3:
                        outer = pltpu.roll(state[f, a + 2, 8 * g : 8 * g + 8, tile(0)], 64, 1)
                        dx[f][g] = jnp.where(lane >= 64, x - outer, zero)
            for g in range(2):
                def rows(f, base=0):
                    return pl.ds(pl.multiple_of(row[f] - base + a * 16 + 8 * g, 8), 8)

                gx = [slope_x[f, a, 8 * g : 8 * g + 8, here] for f in range(4)]
                gy = {f: slope_y[rows(f), here] for f in (2, 0)}
                gz = {f: slope_z[rows(f, 128), here] for f in (0, 3)}
                rate = [
                    MACH * gx[0] + gx[1] + gy[2] + gz[3],
                    MACH * gx[1] + gx[0],
                    MACH * gx[2] + gy[0],
                    MACH * gx[3] + gz[0],
                ]
                for f in range(4):
                    rate[f] = rate[f] + size_y * dy[f][g] + size_z * dz[f][g]
                rate[0] = rate[0] + sign_y * dy[2][g] + sign_z * dz[3][g]
                rate[2] = rate[2] + sign_y * dy[0][g]
                rate[3] = rate[3] + sign_z * dz[0][g]
                if t in (0, 3):
                    s = -1.0 if t == 0 else 1.0
                    d = [dx[f][g] for f in range(4)]
                    own = -HALF_LIFT * (s * MACH + ALPHA)
                    rate[0] = rate[0] + own * d[0] - (HALF_LIFT * s) * d[1]
                    rate[1] = rate[1] + own * d[1] - (HALF_LIFT * s) * d[0]
                    rate[2] = rate[2] + own * d[2]
                    rate[3] = rate[3] + own * d[3]
                new = [q[f][g] + TIME_STEP * rate[f] for f in range(4)]
                source = ground[pl.ds(pl.multiple_of(a * 16 + 8 * g, 8), 8), here]
                new[0] = new[0] + (TIME_STEP * SOURCE_GAIN) * source
                for f in range(4):
                    out_ref[f, a, 8 * g : 8 * g + 8, here] = new[f]
        return carry

    lax.fori_loop(0, 8, step, 0, unroll=2)


def finish_kernel(
    arrival_ref, adj_ref, new_ref, cross_two, cross_one, along_two, along_one, received_ref,
    next_hbm, kappa_hbm, next_ref, kappa_ref, edge, side, sems,
):
    lift = TIME_STEP * HALF_LIFT
    lane = lanes((4, 128))
    j = (lane >> 3) & 7

    def arrived(axis, one, two, s, f, index):
        use_one = is_even(axis) if s > 0 else jnp.logical_not(is_even(axis))
        return jnp.where(use_one, one[(f, *index)], two[(f, *index)])

    def along_terms(s, rows):
        q = [arrived("along", along_one, along_two, s, f, (rows, slice(None))) for f in range(4)]
        q = [pltpu.roll(x, 64, 1) for x in q]
        own = lift * (s * MACH + ALPHA)
        return [own * q[0] + (lift * s) * q[1], own * q[1] + (lift * s) * q[0], own * q[2], own * q[3]]

    def cross_terms(s, t):
        q = [arrived("cross", cross_one, cross_two, s, f, (slice(None), tile(t))) for f in range(4)]
        own = lift * ALPHA
        return [
            own * q[0] + (lift * s) * q[2], own * q[1], own * q[2] + (lift * s) * q[0], own * q[3],
        ]

    for c in range(4):
        rows = slice(4 * c, 4 * c + 4)
        low = along_terms(-1.0, rows)
        high = along_terms(1.0, rows)
        for f in range(4):
            edge[0, f, rows, :] = jnp.where(lane < 64, low[f], 0.0)
            edge[1, f, rows, :] = jnp.where(lane >= 64, high[f], 0.0)
    for t in range(4):
        low = cross_terms(-1.0, t)
        high = cross_terms(1.0, t)
        for f in range(4):
            side[0, f, :, tile(t)] = low[f]
            side[1, f, :, tile(t)] = high[f]
    writes = []
    for f in range(4):
        for t in range(4):
            for a in range(8):
                for c in range(4):
                    value = new_ref[f, a, 4 * c : 4 * c + 4, tile(t)]
                    if c == 0:
                        beyond = pltpu.roll(side[0, f, :, tile(t)], (128 - 8 * a) % 128, 1)
                        value = value + jnp.where(j == 0, beyond, 0.0)
                    if c == 3:
                        beyond = pltpu.roll(side[1, f, :, tile(t)], (56 - 8 * a) % 128, 1)
                        value = value + jnp.where(j == 7, beyond, 0.0)
                    if t == 0 and a == 0:
                        value = value + edge[0, f, 4 * c : 4 * c + 4, :]
                    if t == 3 and a == 7:
                        value = value + edge[1, f, 4 * c : 4 * c + 4, :]
                    next_ref[f, a, c, :, tile(t)] = value
        writes.append(pltpu.make_async_copy(next_ref.at[f], next_hbm.at[f], sems.at[f]))
        writes[f].start()
    for a in range(8):
        for c in range(4):
            q = arrival_ref[a, c]
            clipped = jnp.maximum(q, 0)
            holder = clipped >> 1
            second = (clipped & 1) == 1
            block = jnp.where(second, received_ref[holder, 4:8, :], received_ref[holder, 0:4, :])
            value = TIME_STEP * adj_ref[0, a, c] * block
            kappa_ref[a, c] = jnp.where(q >= 0, value, 0.0)
    writes.append(pltpu.make_async_copy(kappa_ref, kappa_hbm, sems.at[4]))
    writes[4].start()
    for write in writes:
        write.wait()


VMEM = pl.BlockSpec(memory_space=pltpu.VMEM)
HBM = pl.BlockSpec(memory_space=pltpu.HBM)
SMEM = pl.BlockSpec(memory_space=pltpu.SMEM)


def kernel(body, out_shape, in_specs, scratch, flops, moved, out_specs=None, limit=VMEM_BYTES):
    return pl.pallas_call(
        body,
        out_shape=out_shape,
        in_specs=in_specs,
        out_specs=out_specs or jax.tree.map(lambda _: VMEM, out_shape),
        scratch_shapes=scratch,
        compiler_params=pltpu.CompilerParams(vmem_limit_bytes=limit),
        cost_estimate=pl.CostEstimate(flops=flops, bytes_accessed=moved, transcendentals=0),
    )


def array(*shape):
    return jax.ShapeDtypeStruct(shape, F32)


def exchange(value, axis, start):
    pairs = []
    for i in range(start, lax.axis_size(axis) - 1, 2):
        pairs += [(i, i + 1), (i + 1, i)]
    return lax.ppermute(value, axis, pairs)


def per_device(adjoint_state, snapshot_store, dispatch_slot, arrival_slot, mic_node, mic_residual):
    rows = jnp.asarray(derivative_rows())
    outgoing, along_one, along_two, cross_one, cross_two = kernel(
        holder_kernel,
        (array(32, 8, 512), array(4, 16, 128), array(4, 16, 128), array(4, 4, 512), array(4, 4, 512)),
        [HBM] * 4,
        [
            pltpu.SMEM((64,), jnp.int32),
            pltpu.VMEM((64, 3, 4, 512), F32),
            pltpu.VMEM((64, 128), F32),
            pltpu.VMEM((2, 512, 256), BF16),
            pltpu.VMEM((2, 4, 4, 4, 128), F32),
            pltpu.VMEM((2, 4, 8, 4, 512), F32),
            pltpu.VMEM((3, 16, 16, 512), F32),
            pltpu.VMEM((2, 256, 512), BF16),
            pltpu.VMEM((2, 256, 512), BF16),
            pltpu.VMEM((32, 8, 512), F32),
            pltpu.SemaphoreType.DMA((9,)),
        ],
        3_000_000_000, 5_000_000,
        (HBM, VMEM, VMEM, VMEM, VMEM),
        HOLDER_BYTES,
    )(dispatch_slot, adjoint_state, snapshot_store, rows)
    received = lax.all_to_all(outgoing, "cross", split_axis=0, concat_axis=0, tiled=True)
    along_one = exchange(along_one, "along", 0)
    along_two = exchange(along_two, "along", 1)
    cross_one = exchange(cross_one, "cross", 0)
    cross_two = exchange(cross_two, "cross", 1)
    updated = kernel(
        volume_kernel,
        array(4, 8, 16, 512),
        [VMEM] * 4,
        [
            pltpu.VMEM((2, 512, 256), BF16),
            pltpu.VMEM((4, 10, 16, 512), F32),
            pltpu.VMEM((384, 512), BF16),
            pltpu.VMEM((384, 512), BF16),
            pltpu.VMEM((4, 8, 16, 512), F32),
            pltpu.VMEM((256, 512), F32),
            pltpu.VMEM((256, 512), F32),
            pltpu.VMEM((128, 512), F32),
        ],
        4_000_000_000, 4_000_000,
    )(mic_node.reshape(1, 128), mic_residual.reshape(1, 128), adjoint_state, rows)
    return kernel(
        finish_kernel,
        (array(4, 8, 4, 4, 512), array(8, 4, 4, 512)),
        [SMEM] + [VMEM] * 7,
        [
            pltpu.VMEM((4, 8, 4, 4, 512), F32),
            pltpu.VMEM((8, 4, 4, 512), F32),
            pltpu.VMEM((2, 4, 16, 128), F32),
            pltpu.VMEM((2, 4, 4, 512), F32),
            pltpu.SemaphoreType.DMA((5,)),
        ],
        10_000_000, 4_000_000,
        (HBM, HBM),
    )(
        arrival_slot, adjoint_state, updated, cross_two, cross_one, along_two, along_one, received
    )


def solution(mesh):
    in_specs = (
        P(None, "along", "cross", None, None),
        P(("along", "cross"), None, None, None),
        P(("along", "cross")),
        P("along", "cross"),
        P(("along", "cross")),
        P(("along", "cross")),
    )
    out_specs = (P(None, "along", "cross", None, None), P("along", "cross", None, None))
    return jax.shard_map(
        per_device, mesh=mesh, in_specs=in_specs, out_specs=out_specs, check_vma=False
    )
```

```python
import jax
import jax.numpy as jnp
import numpy as np
from jax import lax
from jax.experimental import pallas as pl
from jax.experimental.pallas import tpu as pltpu
from jax.sharding import PartitionSpec as P

MACH = 0.3
ALPHA = 1.3
LIFT_SCALE = 56.0
TIME_STEP = 0.004
SOURCE_GAIN = 50.0
HALF_LIFT = 0.5 * LIFT_SCALE
LOBATTO_INNER = [
    -0.8717401485096066,
    -0.5917001814331423,
    -0.2092992179024789,
    0.2092992179024789,
    0.5917001814331423,
    0.8717401485096066,
]
F32 = jnp.float32
BF16 = jnp.bfloat16
VMEM_BYTES = 24 * 1024 * 1024
HOLDER_BYTES = 60_000_000


def legendre_seven(points):
    previous = points * 0.0 + 1.0
    current = points * 1.0
    for degree_index in range(1, 7):
        following = ((2 * degree_index + 1) * points * current - degree_index * previous) / (
            degree_index + 1
        )
        previous, current = (current, following)
    return current


def derivative_rows():
    degree = 7
    points = np.array([-1.0] + LOBATTO_INNER + [1.0])
    values = legendre_seven(points)
    differ = points[:, None] - points[None, :] + np.eye(degree + 1)
    matrix = values[:, None] / values[None, :] / differ
    matrix = matrix * (1.0 - np.eye(degree + 1))
    matrix[0, 0] = -degree * (degree + 1) / 4.0
    matrix[degree, degree] = degree * (degree + 1) / 4.0
    twice = 2.0 * matrix
    half = np.arange(128) // 64
    along = np.zeros((4, 4, 2, 128))
    for t in range(4):
        for source in range(4):
            along[t, source, 0] = twice[2 * t + half, 2 * source + half]
            along[t, source, 1] = twice[2 * t + half, 2 * source + 1 - half]
    rows = np.stack([np.tile(np.repeat(twice.T, 8, axis=1), 2), np.tile(twice.T, 16)]).astype(np.float32)
    high = rows.astype(BF16)
    low = (rows - high.astype(np.float32)).astype(BF16)
    parts = [along.reshape(32, 128), *high, *low]
    return np.concatenate([part.astype(np.float32) for part in parts])


def along_slope(x, rows_ref):
    turned = [pltpu.roll(value, 64, 1) for value in x]
    slopes = []
    for t in range(4):
        slope = None
        for s in range(4):
            n = 8 * t + 2 * s
            term = rows_ref[n : n + 1, :] * x[s] + rows_ref[n + 1 : n + 2, :] * turned[s]
            slope = term if slope is None else slope + term
        slopes.append(slope)
    return slopes


def fill_table(rows_ref, table):
    lane = lanes((16, 128))
    sub = lax.broadcasted_iota(jnp.int32, (16, 128), 0)
    zero = jnp.zeros((16, 128), F32)
    table[...] = jnp.zeros((2, 512, 256), BF16)
    for h in range(2):
        base = 32 + 16 * h
        row = rows_ref[base + 8 : base + 16, :]
        vertical = jnp.concatenate([row, row], axis=0)
        for g in range(16):
            here = tile(g // 8)
            j = base + 2 * g % 8
            row = jnp.where(sub >= 8, rows_ref[j + 1 : j + 2, :], rows_ref[j : j + 1, :])
            inside = ((lane >> 6) == g // 4 % 2) & ((lane & 7) == (sub & 7))
            table[h, 16 * g : 16 * g + 16, here] = jnp.where(inside, row, zero).astype(BF16)
            inside = (lane >> 3) == (sub >> 3) + 2 * (g % 8)
            table[h, 256 + 16 * g : 272 + 16 * g, here] = jnp.where(inside, vertical, zero).astype(BF16)


def split(x):
    high = x.astype(BF16)
    return high, (x - high.astype(F32)).astype(BF16)


def product(high, low, table_high, table_low):
    def dot(a, b):
        return jnp.dot(a, b, preferred_element_type=F32)

    return dot(high, table_high) + (dot(low, table_high) + dot(high, table_low))


def lanes(shape):
    return lax.broadcasted_iota(jnp.int32, shape, len(shape) - 1)


def tile(t):
    return slice(128 * t, 128 * t + 128)


def is_even(axis):
    return (lax.axis_index(axis) & 1) == 0


def holder_kernel(
    slot_hbm, store_hbm, rows_hbm,
    out_hbm,
    slot_ref, store_ref, rows_ref, table, stage, high, low, total, sems,
):
    pieces = [
        (slot_hbm, slot_ref),
        (store_hbm, store_ref),
        (rows_hbm, rows_ref),
    ]
    copies = [pltpu.make_async_copy(src, dst, sems.at[n]) for n, (src, dst) in enumerate(pieces)]
    for copy in copies:
        copy.start()
    copies[2].wait()
    fill_table(rows_ref, table)
    copies[0].wait()
    copies[1].wait()

    def gather(g, carry):
        rows = pl.ds(pl.multiple_of(g * 16, 16), 16)
        for m in range(4):
            slot = slot_ref[4 * g + m]
            for f in range(3):
                stage[f, g, 4 * m : 4 * m + 4, :] = store_ref[slot, f]
        slopes = along_slope([stage[0, g, :, tile(t)] for t in range(4)], rows_ref)
        for t in range(4):
            total[pl.ds(2 * g, 2), :, tile(t)] = slopes[t].reshape(2, 8, 128)
        for f in range(2):
            high[f, rows], low[f, rows] = split(stage[f + 1, g])
        return carry

    lax.fori_loop(0, 16, gather, 0, unroll=16)
    writes = []
    for c in range(2):
        part = slice(256 * c, 256 * c + 256)
        spread = product(high[0, :, part], low[0, :, part], table[0, 0:256], table[1, 0:256])
        spread += product(high[1, :, part], low[1, :, part], table[0, 256:512], table[1, 256:512])
        total[:, :, part] += spread.reshape(32, 8, 256)
        writes.append(
            pltpu.make_async_copy(total.at[:, :, part], out_hbm.at[:, :, part], sems.at[3 + c])
        )
        writes[c].start()
    for write in writes:
        write.wait()


def trace_kernel(adj_ref, along_one, along_two, cross_one, cross_two):
    even = is_even("along")
    for f in range(4):
        for c in range(4):
            rows = slice(4 * c, 4 * c + 4)
            first = adj_ref[f, 0, c, :, tile(0)]
            last = adj_ref[f, 7, c, :, tile(3)]
            along_one[f, rows, :] = jnp.where(even, last, first)
            along_two[f, rows, :] = jnp.where(even, first, last)
    even = is_even("cross")
    j = (lanes((4, 128)) >> 3) & 7
    for f in range(4):
        for t in range(4):
            last = pltpu.roll(adj_ref[f, 0, 3, :, tile(t)], 72, 1)
            first = adj_ref[f, 0, 0, :, tile(t)]
            for a in range(1, 8):
                other = adj_ref[f, a, 3, :, tile(t)]
                last = jnp.where(j == a, pltpu.roll(other, (72 + 8 * a) % 128, 1), last)
                other = adj_ref[f, a, 0, :, tile(t)]
                first = jnp.where(j == a, pltpu.roll(other, 8 * a, 1), first)
            cross_one[f, :, tile(t)] = jnp.where(even, last, first)
            cross_two[f, :, tile(t)] = jnp.where(even, first, last)


def volume_kernel(
    node_ref, residual_ref, adj_ref, rows_ref, out_ref, table, state, high, low, slope_x, slope_y, slope_z, ground
):
    fill_table(rows_ref, table)
    row = {2: 0, 0: 128, 3: 256}
    state[:, 0] = jnp.zeros((4, 16, 512), F32)
    state[:, 9] = jnp.zeros((4, 16, 512), F32)

    def load(a, carry):
        for f in range(4):
            for c in range(4):
                state[f, a + 1, 4 * c : 4 * c + 4, :] = adj_ref[f, a, c]
            slopes = along_slope([state[f, a + 1, :, tile(t)] for t in range(4)], rows_ref)
            for t in range(4):
                slope_x[f, a, :, tile(t)] = slopes[t]
            if f in row:
                rows = pl.ds(pl.multiple_of(row[f] + a * 16, 16), 16)
                high[rows], low[rows] = split(state[f, a + 1])
        return carry

    lax.fori_loop(0, 8, load, 0, unroll=8)
    for c in range(2):
        part = slice(256 * c, 256 * c + 256)
        slope_y[:, part] = product(high[0:256, part], low[0:256, part], table[0, 0:256], table[1, 0:256])
        slope_z[:, part] = product(
            high[128:384, part], low[128:384, part], table[0, 256:512], table[1, 256:512]
        )

    node = node_ref[...]
    residual = residual_ref[...]
    target = lax.broadcasted_iota(jnp.int32, (128, 128), 0)
    spread = jnp.where(target == 4 * (node >> 6), residual, 0.0)
    place = lax.broadcasted_iota(jnp.int32, (512, 128), 0) == 8 * (node & 63)
    place = jnp.where(place, 1.0, 0.0).astype(BF16)
    ones, rest = split(spread)
    twos = (spread - ones.astype(F32) - rest.astype(F32)).astype(BF16)

    def match(a):
        return lax.dot_general(a, place, (((1,), (1,)), ((), ())), preferred_element_type=F32)

    ground[...] = match(ones) + (match(rest) + match(twos))

    lane = lanes((8, 128))
    sub = lax.broadcasted_iota(jnp.int32, (8, 128), 0)
    j = (lane >> 3) & 7
    k = lane & 7
    e = sub & 3
    odd = sub >= 4
    top_y = j == 7
    top_z = k == 7
    floor = e == 0
    ceiling = e == 3
    zero = jnp.zeros((8, 128), F32)
    sign_y = jnp.where(j == 0, HALF_LIFT, jnp.where(top_y, -HALF_LIFT, 0.0))
    size_y = jnp.where((j == 0) | top_y, -HALF_LIFT * ALPHA, 0.0)
    sign_z = jnp.where(k == 0, HALF_LIFT, jnp.where(top_z, -HALF_LIFT, 0.0))
    size_z = jnp.where((k == 0) | top_z, -HALF_LIFT * ALPHA, 0.0)

    def step(a, carry):
        for t in range(4):
            here = tile(t)
            q = [[state[f, a + 1, 8 * g : 8 * g + 8, here] for g in range(2)] for f in range(4)]
            dy = [[None] * 2 for _ in range(4)]
            dz = [[None] * 2 for _ in range(4)]
            dx = [[None] * 2 for _ in range(4)]
            for f in range(4):
                swap = [pltpu.roll(q[f][g], 4, 0) for g in range(2)]
                before = [jnp.where(odd, swap[0], zero), jnp.where(odd, swap[1], swap[0])]
                after = [jnp.where(odd, swap[1], swap[0]), jnp.where(odd, zero, swap[1])]
                for g in range(2):
                    x = q[f][g]
                    outer = jnp.where(top_y, pltpu.roll(after[g], 56, 1), pltpu.roll(before[g], 72, 1))
                    dy[f][g] = x - outer
                    below = pltpu.roll(pltpu.roll(x, 1, 0), 121, 1)
                    below = jnp.where(floor, -x if f == 3 else x, below)
                    above = pltpu.roll(pltpu.roll(x, 7, 0), 7, 1)
                    above = jnp.where(ceiling, zero, above)
                    dz[f][g] = x - jnp.where(top_z, above, below)
                    if t == 0:
                        outer = pltpu.roll(state[f, a, 8 * g : 8 * g + 8, tile(3)], 64, 1)
                        dx[f][g] = jnp.where(lane < 64, x - outer, zero)
                    if t == 3:
                        outer = pltpu.roll(state[f, a + 2, 8 * g : 8 * g + 8, tile(0)], 64, 1)
                        dx[f][g] = jnp.where(lane >= 64, x - outer, zero)
            for g in range(2):
                def rows(f, base=0):
                    return pl.ds(pl.multiple_of(row[f] - base + a * 16 + 8 * g, 8), 8)

                gx = [slope_x[f, a, 8 * g : 8 * g + 8, here] for f in range(4)]
                gy = {f: slope_y[rows(f), here] for f in (2, 0)}
                gz = {f: slope_z[rows(f, 128), here] for f in (0, 3)}
                rate = [
                    MACH * gx[0] + gx[1] + gy[2] + gz[3],
                    MACH * gx[1] + gx[0],
                    MACH * gx[2] + gy[0],
                    MACH * gx[3] + gz[0],
                ]
                for f in range(4):
                    rate[f] = rate[f] + size_y * dy[f][g] + size_z * dz[f][g]
                rate[0] = rate[0] + sign_y * dy[2][g] + sign_z * dz[3][g]
                rate[2] = rate[2] + sign_y * dy[0][g]
                rate[3] = rate[3] + sign_z * dz[0][g]
                if t in (0, 3):
                    s = -1.0 if t == 0 else 1.0
                    d = [dx[f][g] for f in range(4)]
                    own = -HALF_LIFT * (s * MACH + ALPHA)
                    rate[0] = rate[0] + own * d[0] - (HALF_LIFT * s) * d[1]
                    rate[1] = rate[1] + own * d[1] - (HALF_LIFT * s) * d[0]
                    rate[2] = rate[2] + own * d[2]
                    rate[3] = rate[3] + own * d[3]
                new = [q[f][g] + TIME_STEP * rate[f] for f in range(4)]
                source = ground[pl.ds(pl.multiple_of(a * 16 + 8 * g, 8), 8), here]
                new[0] = new[0] + (TIME_STEP * SOURCE_GAIN) * source
                for f in range(4):
                    out_ref[f, a, 8 * g : 8 * g + 8, here] = new[f]
        return carry

    lax.fori_loop(0, 8, step, 0, unroll=2)


def finish_kernel(
    arrival_ref, adj_ref, new_ref, cross_two, cross_one, along_two, along_one, received_ref,
    next_hbm, kappa_hbm, next_ref, kappa_ref, edge, side, sems,
):
    lift = TIME_STEP * HALF_LIFT
    lane = lanes((4, 128))
    j = (lane >> 3) & 7

    def arrived(axis, one, two, s, f, index):
        use_one = is_even(axis) if s > 0 else jnp.logical_not(is_even(axis))
        return jnp.where(use_one, one[(f, *index)], two[(f, *index)])

    def along_terms(s, rows):
        q = [arrived("along", along_one, along_two, s, f, (rows, slice(None))) for f in range(4)]
        q = [pltpu.roll(x, 64, 1) for x in q]
        own = lift * (s * MACH + ALPHA)
        return [own * q[0] + (lift * s) * q[1], own * q[1] + (lift * s) * q[0], own * q[2], own * q[3]]

    def cross_terms(s, t):
        q = [arrived("cross", cross_one, cross_two, s, f, (slice(None), tile(t))) for f in range(4)]
        own = lift * ALPHA
        return [
            own * q[0] + (lift * s) * q[2], own * q[1], own * q[2] + (lift * s) * q[0], own * q[3],
        ]

    for c in range(4):
        rows = slice(4 * c, 4 * c + 4)
        low = along_terms(-1.0, rows)
        high = along_terms(1.0, rows)
        for f in range(4):
            edge[0, f, rows, :] = jnp.where(lane < 64, low[f], 0.0)
            edge[1, f, rows, :] = jnp.where(lane >= 64, high[f], 0.0)
    for t in range(4):
        low = cross_terms(-1.0, t)
        high = cross_terms(1.0, t)
        for f in range(4):
            side[0, f, :, tile(t)] = low[f]
            side[1, f, :, tile(t)] = high[f]
    writes = []
    for f in range(4):
        for t in range(4):
            for a in range(8):
                for c in range(4):
                    value = new_ref[f, a, 4 * c : 4 * c + 4, tile(t)]
                    if c == 0:
                        beyond = pltpu.roll(side[0, f, :, tile(t)], (128 - 8 * a) % 128, 1)
                        value = value + jnp.where(j == 0, beyond, 0.0)
                    if c == 3:
                        beyond = pltpu.roll(side[1, f, :, tile(t)], (56 - 8 * a) % 128, 1)
                        value = value + jnp.where(j == 7, beyond, 0.0)
                    if t == 0 and a == 0:
                        value = value + edge[0, f, 4 * c : 4 * c + 4, :]
                    if t == 3 and a == 7:
                        value = value + edge[1, f, 4 * c : 4 * c + 4, :]
                    next_ref[f, a, c, :, tile(t)] = value
        writes.append(pltpu.make_async_copy(next_ref.at[f], next_hbm.at[f], sems.at[f]))
        writes[f].start()
    for a in range(8):
        for c in range(4):
            q = arrival_ref[a, c]
            clipped = jnp.maximum(q, 0)
            holder = clipped >> 1
            second = (clipped & 1) == 1
            block = jnp.where(second, received_ref[holder, 4:8, :], received_ref[holder, 0:4, :])
            value = TIME_STEP * adj_ref[0, a, c] * block
            kappa_ref[a, c] = jnp.where(q >= 0, value, 0.0)
    writes.append(pltpu.make_async_copy(kappa_ref, kappa_hbm, sems.at[4]))
    writes[4].start()
    for write in writes:
        write.wait()


VMEM = pl.BlockSpec(memory_space=pltpu.VMEM)
HBM = pl.BlockSpec(memory_space=pltpu.HBM)
SMEM = pl.BlockSpec(memory_space=pltpu.SMEM)


def kernel(body, out_shape, in_specs, scratch, flops, moved, out_specs=None, limit=VMEM_BYTES):
    return pl.pallas_call(
        body,
        out_shape=out_shape,
        in_specs=in_specs,
        out_specs=out_specs or jax.tree.map(lambda _: VMEM, out_shape),
        scratch_shapes=scratch,
        compiler_params=pltpu.CompilerParams(vmem_limit_bytes=limit),
        cost_estimate=pl.CostEstimate(flops=flops, bytes_accessed=moved, transcendentals=0),
    )


def array(*shape):
    return jax.ShapeDtypeStruct(shape, F32)


def exchange(value, axis, start):
    pairs = []
    for i in range(start, lax.axis_size(axis) - 1, 2):
        pairs += [(i, i + 1), (i + 1, i)]
    return lax.ppermute(value, axis, pairs)


def per_device(adjoint_state, snapshot_store, dispatch_slot, arrival_slot, mic_node, mic_residual):
    rows = jnp.asarray(derivative_rows())
    outgoing = kernel(
        holder_kernel,
        array(32, 8, 512),
        [HBM] * 3,
        [
            pltpu.SMEM((64,), jnp.int32),
            pltpu.VMEM((64, 3, 4, 512), F32),
            pltpu.VMEM((64, 128), F32),
            pltpu.VMEM((2, 512, 256), BF16),
            pltpu.VMEM((3, 16, 16, 512), F32),
            pltpu.VMEM((2, 256, 512), BF16),
            pltpu.VMEM((2, 256, 512), BF16),
            pltpu.VMEM((32, 8, 512), F32),
            pltpu.SemaphoreType.DMA((5,)),
        ],
        3_000_000_000, 5_000_000,
        HBM,
        HOLDER_BYTES,
    )(dispatch_slot, snapshot_store, rows)
    received = lax.all_to_all(outgoing, "cross", split_axis=0, concat_axis=0, tiled=True)
    along_one, along_two, cross_one, cross_two = kernel(
        trace_kernel,
        (array(4, 16, 128), array(4, 16, 128), array(4, 4, 512), array(4, 4, 512)),
        [VMEM],
        [],
        1_000_000, 500_000,
    )(adjoint_state)
    updated = kernel(
        volume_kernel,
        array(4, 8, 16, 512),
        [VMEM] * 4,
        [
            pltpu.VMEM((2, 512, 256), BF16),
            pltpu.VMEM((4, 10, 16, 512), F32),
            pltpu.VMEM((384, 512), BF16),
            pltpu.VMEM((384, 512), BF16),
            pltpu.VMEM((4, 8, 16, 512), F32),
            pltpu.VMEM((256, 512), F32),
            pltpu.VMEM((256, 512), F32),
            pltpu.VMEM((128, 512), F32),
        ],
        4_000_000_000, 4_000_000,
    )(mic_node.reshape(1, 128), mic_residual.reshape(1, 128), adjoint_state, rows)
    along_one = exchange(along_one, "along", 0)
    along_two = exchange(along_two, "along", 1)
    cross_one = exchange(cross_one, "cross", 0)
    cross_two = exchange(cross_two, "cross", 1)
    return kernel(
        finish_kernel,
        (array(4, 8, 4, 4, 512), array(8, 4, 4, 512)),
        [SMEM] + [VMEM] * 7,
        [
            pltpu.VMEM((4, 8, 4, 4, 512), F32),
            pltpu.VMEM((8, 4, 4, 512), F32),
            pltpu.VMEM((2, 4, 16, 128), F32),
            pltpu.VMEM((2, 4, 4, 512), F32),
            pltpu.SemaphoreType.DMA((5,)),
        ],
        10_000_000, 4_000_000,
        (HBM, HBM),
    )(
        arrival_slot, adjoint_state, updated, cross_two, cross_one, along_two, along_one, received
    )


def solution(mesh):
    in_specs = (
        P(None, "along", "cross", None, None),
        P(("along", "cross"), None, None, None),
        P(("along", "cross")),
        P("along", "cross"),
        P(("along", "cross")),
        P(("along", "cross")),
    )
    out_specs = (P(None, "along", "cross", None, None), P("along", "cross", None, None))
    return jax.shard_map(
        per_device, mesh=mesh, in_specs=in_specs, out_specs=out_specs, check_vma=False
    )
```

```python
import jax
import jax.numpy as jnp
import numpy as np
from jax import lax
from jax.experimental import pallas as pl
from jax.experimental.pallas import tpu as pltpu
from jax.sharding import PartitionSpec as P

MACH = 0.3
ALPHA = 1.3
LIFT_SCALE = 56.0
TIME_STEP = 0.004
SOURCE_GAIN = 50.0
HALF_LIFT = 0.5 * LIFT_SCALE
LOBATTO_INNER = [
    -0.8717401485096066,
    -0.5917001814331423,
    -0.2092992179024789,
    0.2092992179024789,
    0.5917001814331423,
    0.8717401485096066,
]
F32 = jnp.float32
BF16 = jnp.bfloat16
VMEM_BYTES = 24 * 1024 * 1024
HOLDER_BYTES = 60_000_000


def legendre_seven(points):
    previous = points * 0.0 + 1.0
    current = points * 1.0
    for degree_index in range(1, 7):
        following = ((2 * degree_index + 1) * points * current - degree_index * previous) / (
            degree_index + 1
        )
        previous, current = (current, following)
    return current


def derivative_rows():
    degree = 7
    points = np.array([-1.0] + LOBATTO_INNER + [1.0])
    values = legendre_seven(points)
    differ = points[:, None] - points[None, :] + np.eye(degree + 1)
    matrix = values[:, None] / values[None, :] / differ
    matrix = matrix * (1.0 - np.eye(degree + 1))
    matrix[0, 0] = -degree * (degree + 1) / 4.0
    matrix[degree, degree] = degree * (degree + 1) / 4.0
    twice = 2.0 * matrix
    half = np.arange(128) // 64
    along = np.zeros((4, 4, 2, 128))
    for t in range(4):
        for source in range(4):
            along[t, source, 0] = twice[2 * t + half, 2 * source + half]
            along[t, source, 1] = twice[2 * t + half, 2 * source + 1 - half]
    rows = np.stack([np.tile(np.repeat(twice.T, 8, axis=1), 2), np.tile(twice.T, 16)]).astype(np.float32)
    high = rows.astype(BF16)
    low = (rows - high.astype(np.float32)).astype(BF16)
    parts = [along.reshape(32, 128), *high, *low]
    return np.concatenate([part.astype(np.float32) for part in parts])


def along_slope(x, rows_ref):
    turned = [pltpu.roll(value, 64, 1) for value in x]
    slopes = []
    for t in range(4):
        slope = None
        for s in range(4):
            n = 8 * t + 2 * s
            term = rows_ref[n : n + 1, :] * x[s] + rows_ref[n + 1 : n + 2, :] * turned[s]
            slope = term if slope is None else slope + term
        slopes.append(slope)
    return slopes


def fill_table(rows_ref, table):
    lane = lanes((16, 128))
    sub = lax.broadcasted_iota(jnp.int32, (16, 128), 0)
    zero = jnp.zeros((16, 128), F32)
    table[...] = jnp.zeros((2, 512, 256), BF16)
    for h in range(2):
        base = 32 + 16 * h
        row = rows_ref[base + 8 : base + 16, :]
        vertical = jnp.concatenate([row, row], axis=0)
        for g in range(16):
            here = tile(g // 8)
            j = base + 2 * g % 8
            row = jnp.where(sub >= 8, rows_ref[j + 1 : j + 2, :], rows_ref[j : j + 1, :])
            inside = ((lane >> 6) == g // 4 % 2) & ((lane & 7) == (sub & 7))
            table[h, 16 * g : 16 * g + 16, here] = jnp.where(inside, row, zero).astype(BF16)
            inside = (lane >> 3) == (sub >> 3) + 2 * (g % 8)
            table[h, 256 + 16 * g : 272 + 16 * g, here] = jnp.where(inside, vertical, zero).astype(BF16)


def split(x):
    high = x.astype(BF16)
    return high, (x - high.astype(F32)).astype(BF16)


def product(high, low, table_high, table_low):
    def dot(a, b):
        return jnp.dot(a, b, preferred_element_type=F32)

    return dot(high, table_high) + (dot(low, table_high) + dot(high, table_low))


def lanes(shape):
    return lax.broadcasted_iota(jnp.int32, shape, len(shape) - 1)


def tile(t):
    return slice(128 * t, 128 * t + 128)


def is_even(axis):
    return (lax.axis_index(axis) & 1) == 0


def holder_kernel(
    slot_hbm, store_hbm, rows_hbm,
    out_hbm,
    slot_ref, store_ref, rows_ref, table, stage, high, low, total, sems,
):
    pieces = [
        (slot_hbm, slot_ref),
        (store_hbm, store_ref),
        (rows_hbm, rows_ref),
    ]
    copies = [pltpu.make_async_copy(src, dst, sems.at[n]) for n, (src, dst) in enumerate(pieces)]
    for copy in copies:
        copy.start()
    copies[2].wait()
    fill_table(rows_ref, table)
    copies[0].wait()
    copies[1].wait()

    def gather(g, carry):
        rows = pl.ds(pl.multiple_of(g * 16, 16), 16)
        for m in range(4):
            slot = slot_ref[4 * g + m]
            for f in range(3):
                stage[f, g, 4 * m : 4 * m + 4, :] = store_ref[slot, f]
        slopes = along_slope([stage[0, g, :, tile(t)] for t in range(4)], rows_ref)
        for t in range(4):
            total[pl.ds(2 * g, 2), :, tile(t)] = slopes[t].reshape(2, 8, 128)
        for f in range(2):
            high[f, rows], low[f, rows] = split(stage[f + 1, g])
        return carry

    lax.fori_loop(0, 16, gather, 0, unroll=16)
    writes = []
    for c in range(2):
        part = slice(256 * c, 256 * c + 256)
        spread = product(high[0, :, part], low[0, :, part], table[0, 0:256], table[1, 0:256])
        spread += product(high[1, :, part], low[1, :, part], table[0, 256:512], table[1, 256:512])
        total[:, :, part] += spread.reshape(32, 8, 256)
        writes.append(
            pltpu.make_async_copy(total.at[:, :, part], out_hbm.at[:, :, part], sems.at[3 + c])
        )
        writes[c].start()
    for write in writes:
        write.wait()


def trace_kernel(adj_ref, along_one, along_two, cross_one, cross_two):
    even = is_even("along")
    for f in range(4):
        for c in range(4):
            rows = slice(4 * c, 4 * c + 4)
            first = adj_ref[f, 0, c, :, tile(0)]
            last = adj_ref[f, 7, c, :, tile(3)]
            along_one[f, rows, :] = jnp.where(even, last, first)
            along_two[f, rows, :] = jnp.where(even, first, last)
    even = is_even("cross")
    j = (lanes((4, 128)) >> 3) & 7
    for f in range(4):
        for t in range(4):
            last = pltpu.roll(adj_ref[f, 0, 3, :, tile(t)], 72, 1)
            first = adj_ref[f, 0, 0, :, tile(t)]
            for a in range(1, 8):
                other = adj_ref[f, a, 3, :, tile(t)]
                last = jnp.where(j == a, pltpu.roll(other, (72 + 8 * a) % 128, 1), last)
                other = adj_ref[f, a, 0, :, tile(t)]
                first = jnp.where(j == a, pltpu.roll(other, 8 * a, 1), first)
            cross_one[f, :, tile(t)] = jnp.where(even, last, first)
            cross_two[f, :, tile(t)] = jnp.where(even, first, last)


def volume_kernel(
    node_ref, residual_ref, adj_ref, rows_ref, out_ref, table, state, high, low, slope_x, slope_y, slope_z, ground
):
    fill_table(rows_ref, table)
    row = {2: 0, 0: 128, 3: 256}
    state[:, 0] = jnp.zeros((4, 16, 512), F32)
    state[:, 9] = jnp.zeros((4, 16, 512), F32)

    def load(a, carry):
        for f in range(4):
            for c in range(4):
                state[f, a + 1, 4 * c : 4 * c + 4, :] = adj_ref[f, a, c]
            slopes = along_slope([state[f, a + 1, :, tile(t)] for t in range(4)], rows_ref)
            for t in range(4):
                slope_x[f, a, :, tile(t)] = slopes[t]
            if f in row:
                rows = pl.ds(pl.multiple_of(row[f] + a * 16, 16), 16)
                high[rows], low[rows] = split(state[f, a + 1])
        return carry

    lax.fori_loop(0, 8, load, 0, unroll=8)
    for c in range(2):
        part = slice(256 * c, 256 * c + 256)
        slope_y[:, part] = product(high[0:256, part], low[0:256, part], table[0, 0:256], table[1, 0:256])
        slope_z[:, part] = product(
            high[128:384, part], low[128:384, part], table[0, 256:512], table[1, 256:512]
        )

    node = node_ref[...]
    residual = residual_ref[...]
    target = lax.broadcasted_iota(jnp.int32, (128, 128), 0)
    spread = jnp.where(target == 4 * (node >> 6), residual, 0.0)
    place = lax.broadcasted_iota(jnp.int32, (512, 128), 0) == 8 * (node & 63)
    place = jnp.where(place, 1.0, 0.0).astype(BF16)
    ones, rest = split(spread)
    twos = (spread - ones.astype(F32) - rest.astype(F32)).astype(BF16)

    def match(a):
        return lax.dot_general(a, place, (((1,), (1,)), ((), ())), preferred_element_type=F32)

    ground[...] = match(ones) + (match(rest) + match(twos))

    lane = lanes((8, 128))
    sub = lax.broadcasted_iota(jnp.int32, (8, 128), 0)
    j = (lane >> 3) & 7
    k = lane & 7
    e = sub & 3
    odd = sub >= 4
    top_y = j == 7
    top_z = k == 7
    floor = e == 0
    ceiling = e == 3
    zero = jnp.zeros((8, 128), F32)
    sign_y = jnp.where(j == 0, HALF_LIFT, jnp.where(top_y, -HALF_LIFT, 0.0))
    size_y = jnp.where((j == 0) | top_y, -HALF_LIFT * ALPHA, 0.0)
    sign_z = jnp.where(k == 0, HALF_LIFT, jnp.where(top_z, -HALF_LIFT, 0.0))
    size_z = jnp.where((k == 0) | top_z, -HALF_LIFT * ALPHA, 0.0)

    def step(a, carry):
        for t in range(4):
            here = tile(t)
            q = [[state[f, a + 1, 8 * g : 8 * g + 8, here] for g in range(2)] for f in range(4)]
            dy = [[None] * 2 for _ in range(4)]
            dz = [[None] * 2 for _ in range(4)]
            dx = [[None] * 2 for _ in range(4)]
            for f in range(4):
                swap = [pltpu.roll(q[f][g], 4, 0) for g in range(2)]
                before = [jnp.where(odd, swap[0], zero), jnp.where(odd, swap[1], swap[0])]
                after = [jnp.where(odd, swap[1], swap[0]), jnp.where(odd, zero, swap[1])]
                for g in range(2):
                    x = q[f][g]
                    outer = jnp.where(top_y, pltpu.roll(after[g], 56, 1), pltpu.roll(before[g], 72, 1))
                    dy[f][g] = x - outer
                    below = pltpu.roll(pltpu.roll(x, 1, 0), 121, 1)
                    below = jnp.where(floor, -x if f == 3 else x, below)
                    above = pltpu.roll(pltpu.roll(x, 7, 0), 7, 1)
                    above = jnp.where(ceiling, zero, above)
                    dz[f][g] = x - jnp.where(top_z, above, below)
                    if t == 0:
                        outer = pltpu.roll(state[f, a, 8 * g : 8 * g + 8, tile(3)], 64, 1)
                        dx[f][g] = jnp.where(lane < 64, x - outer, zero)
                    if t == 3:
                        outer = pltpu.roll(state[f, a + 2, 8 * g : 8 * g + 8, tile(0)], 64, 1)
                        dx[f][g] = jnp.where(lane >= 64, x - outer, zero)
            for g in range(2):
                def rows(f, base=0):
                    return pl.ds(pl.multiple_of(row[f] - base + a * 16 + 8 * g, 8), 8)

                gx = [slope_x[f, a, 8 * g : 8 * g + 8, here] for f in range(4)]
                gy = {f: slope_y[rows(f), here] for f in (2, 0)}
                gz = {f: slope_z[rows(f, 128), here] for f in (0, 3)}
                rate = [
                    MACH * gx[0] + gx[1] + gy[2] + gz[3],
                    MACH * gx[1] + gx[0],
                    MACH * gx[2] + gy[0],
                    MACH * gx[3] + gz[0],
                ]
                for f in range(4):
                    rate[f] = rate[f] + size_y * dy[f][g] + size_z * dz[f][g]
                rate[0] = rate[0] + sign_y * dy[2][g] + sign_z * dz[3][g]
                rate[2] = rate[2] + sign_y * dy[0][g]
                rate[3] = rate[3] + sign_z * dz[0][g]
                if t in (0, 3):
                    s = -1.0 if t == 0 else 1.0
                    d = [dx[f][g] for f in range(4)]
                    own = -HALF_LIFT * (s * MACH + ALPHA)
                    rate[0] = rate[0] + own * d[0] - (HALF_LIFT * s) * d[1]
                    rate[1] = rate[1] + own * d[1] - (HALF_LIFT * s) * d[0]
                    rate[2] = rate[2] + own * d[2]
                    rate[3] = rate[3] + own * d[3]
                new = [q[f][g] + TIME_STEP * rate[f] for f in range(4)]
                source = ground[pl.ds(pl.multiple_of(a * 16 + 8 * g, 8), 8), here]
                new[0] = new[0] + (TIME_STEP * SOURCE_GAIN) * source
                for f in range(4):
                    out_ref[f, a, 8 * g : 8 * g + 8, here] = new[f]
        return carry

    lax.fori_loop(0, 8, step, 0, unroll=8)


def finish_kernel(
    arrival_ref, adj_ref, new_ref, cross_two, along_two, cross_one, along_one, received_ref,
    next_hbm, kappa_hbm, next_ref, kappa_ref, edge, side, sems,
):
    lift = TIME_STEP * HALF_LIFT
    lane = lanes((4, 128))
    j = (lane >> 3) & 7

    def arrived(axis, one, two, s, f, index):
        use_one = is_even(axis) if s > 0 else jnp.logical_not(is_even(axis))
        return jnp.where(use_one, one[(f, *index)], two[(f, *index)])

    def along_terms(s, rows):
        q = [arrived("along", along_one, along_two, s, f, (rows, slice(None))) for f in range(4)]
        q = [pltpu.roll(x, 64, 1) for x in q]
        own = lift * (s * MACH + ALPHA)
        return [own * q[0] + (lift * s) * q[1], own * q[1] + (lift * s) * q[0], own * q[2], own * q[3]]

    def cross_terms(s, t):
        q = [arrived("cross", cross_one, cross_two, s, f, (slice(None), tile(t))) for f in range(4)]
        own = lift * ALPHA
        return [
            own * q[0] + (lift * s) * q[2], own * q[1], own * q[2] + (lift * s) * q[0], own * q[3],
        ]

    for c in range(4):
        rows = slice(4 * c, 4 * c + 4)
        low = along_terms(-1.0, rows)
        high = along_terms(1.0, rows)
        for f in range(4):
            edge[0, f, rows, :] = jnp.where(lane < 64, low[f], 0.0)
            edge[1, f, rows, :] = jnp.where(lane >= 64, high[f], 0.0)
    for t in range(4):
        low = cross_terms(-1.0, t)
        high = cross_terms(1.0, t)
        for f in range(4):
            side[0, f, :, tile(t)] = low[f]
            side[1, f, :, tile(t)] = high[f]
    writes = []
    for f in range(4):
        for t in range(4):
            for a in range(8):
                for c in range(4):
                    value = new_ref[f, a, 4 * c : 4 * c + 4, tile(t)]
                    if c == 0:
                        beyond = pltpu.roll(side[0, f, :, tile(t)], (128 - 8 * a) % 128, 1)
                        value = value + jnp.where(j == 0, beyond, 0.0)
                    if c == 3:
                        beyond = pltpu.roll(side[1, f, :, tile(t)], (56 - 8 * a) % 128, 1)
                        value = value + jnp.where(j == 7, beyond, 0.0)
                    if t == 0 and a == 0:
                        value = value + edge[0, f, 4 * c : 4 * c + 4, :]
                    if t == 3 and a == 7:
                        value = value + edge[1, f, 4 * c : 4 * c + 4, :]
                    next_ref[f, a, c, :, tile(t)] = value
        writes.append(pltpu.make_async_copy(next_ref.at[f], next_hbm.at[f], sems.at[f]))
        writes[f].start()
    for a in range(8):
        for c in range(4):
            q = arrival_ref[a, c]
            clipped = jnp.maximum(q, 0)
            holder = clipped >> 1
            second = (clipped & 1) == 1
            block = jnp.where(second, received_ref[holder, 4:8, :], received_ref[holder, 0:4, :])
            value = TIME_STEP * adj_ref[0, a, c] * block
            kappa_ref[a, c] = jnp.where(q >= 0, value, 0.0)
    writes.append(pltpu.make_async_copy(kappa_ref, kappa_hbm, sems.at[4]))
    writes[4].start()
    for write in writes:
        write.wait()


VMEM = pl.BlockSpec(memory_space=pltpu.VMEM)
HBM = pl.BlockSpec(memory_space=pltpu.HBM)
SMEM = pl.BlockSpec(memory_space=pltpu.SMEM)


def kernel(body, out_shape, in_specs, scratch, flops, moved, out_specs=None, limit=VMEM_BYTES):
    return pl.pallas_call(
        body,
        out_shape=out_shape,
        in_specs=in_specs,
        out_specs=out_specs or jax.tree.map(lambda _: VMEM, out_shape),
        scratch_shapes=scratch,
        compiler_params=pltpu.CompilerParams(vmem_limit_bytes=limit),
        cost_estimate=pl.CostEstimate(flops=flops, bytes_accessed=moved, transcendentals=0),
    )


def array(*shape):
    return jax.ShapeDtypeStruct(shape, F32)


def exchange(value, axis, start):
    pairs = []
    for i in range(start, lax.axis_size(axis) - 1, 2):
        pairs += [(i, i + 1), (i + 1, i)]
    return lax.ppermute(value, axis, pairs)


def per_device(adjoint_state, snapshot_store, dispatch_slot, arrival_slot, mic_node, mic_residual):
    rows = jnp.asarray(derivative_rows())
    outgoing = kernel(
        holder_kernel,
        array(32, 8, 512),
        [HBM] * 3,
        [
            pltpu.SMEM((64,), jnp.int32),
            pltpu.VMEM((64, 3, 4, 512), F32),
            pltpu.VMEM((64, 128), F32),
            pltpu.VMEM((2, 512, 256), BF16),
            pltpu.VMEM((3, 16, 16, 512), F32),
            pltpu.VMEM((2, 256, 512), BF16),
            pltpu.VMEM((2, 256, 512), BF16),
            pltpu.VMEM((32, 8, 512), F32),
            pltpu.SemaphoreType.DMA((5,)),
        ],
        3_000_000_000, 5_000_000,
        HBM,
        HOLDER_BYTES,
    )(dispatch_slot, snapshot_store, rows)
    received = lax.all_to_all(outgoing, "cross", split_axis=0, concat_axis=0, tiled=True)
    along_one, along_two, cross_one, cross_two = kernel(
        trace_kernel,
        (array(4, 16, 128), array(4, 16, 128), array(4, 4, 512), array(4, 4, 512)),
        [VMEM],
        [],
        1_000_000, 500_000,
    )(adjoint_state)
    updated = kernel(
        volume_kernel,
        array(4, 8, 16, 512),
        [VMEM] * 4,
        [
            pltpu.VMEM((2, 512, 256), BF16),
            pltpu.VMEM((4, 10, 16, 512), F32),
            pltpu.VMEM((384, 512), BF16),
            pltpu.VMEM((384, 512), BF16),
            pltpu.VMEM((4, 8, 16, 512), F32),
            pltpu.VMEM((256, 512), F32),
            pltpu.VMEM((256, 512), F32),
            pltpu.VMEM((128, 512), F32),
        ],
        4_000_000_000, 4_000_000,
    )(mic_node.reshape(1, 128), mic_residual.reshape(1, 128), adjoint_state, rows)
    along_one = exchange(along_one, "along", 0)
    along_two = exchange(along_two, "along", 1)
    cross_one = exchange(cross_one, "cross", 0)
    cross_two = exchange(cross_two, "cross", 1)
    return kernel(
        finish_kernel,
        (array(4, 8, 4, 4, 512), array(8, 4, 4, 512)),
        [SMEM] + [VMEM] * 7,
        [
            pltpu.VMEM((4, 8, 4, 4, 512), F32),
            pltpu.VMEM((8, 4, 4, 512), F32),
            pltpu.VMEM((2, 4, 16, 128), F32),
            pltpu.VMEM((2, 4, 4, 512), F32),
            pltpu.SemaphoreType.DMA((5,)),
        ],
        10_000_000, 4_000_000,
        (HBM, HBM),
    )(
        arrival_slot, adjoint_state, updated, cross_two, along_two, cross_one, along_one, received
    )


def solution(mesh):
    in_specs = (
        P(None, "along", "cross", None, None),
        P(("along", "cross"), None, None, None),
        P(("along", "cross")),
        P("along", "cross"),
        P(("along", "cross")),
        P(("along", "cross")),
    )
    out_specs = (P(None, "along", "cross", None, None), P("along", "cross", None, None))
    return jax.shard_map(
        per_device, mesh=mesh, in_specs=in_specs, out_specs=out_specs, check_vma=False
    )
```

```python
import jax
import jax.numpy as jnp
import numpy as np
from jax import lax
from jax.experimental import pallas as pl
from jax.experimental.pallas import tpu as pltpu
from jax.sharding import PartitionSpec as P

MACH = 0.3
ALPHA = 1.3
LIFT_SCALE = 56.0
TIME_STEP = 0.004
SOURCE_GAIN = 50.0
HALF_LIFT = 0.5 * LIFT_SCALE
LOBATTO_INNER = [
    -0.8717401485096066,
    -0.5917001814331423,
    -0.2092992179024789,
    0.2092992179024789,
    0.5917001814331423,
    0.8717401485096066,
]
F32 = jnp.float32
BF16 = jnp.bfloat16
VMEM_BYTES = 24 * 1024 * 1024
PEER_ORDER = (31, 23, 18, 4, 12, 21, 8, 19, 28, 3, 2, 1, 24, 26, 14, 11, 17, 0, 7, 27, 29, 5, 16, 25, 6, 15, 9, 20, 30, 22, 13, 10)
HOLDER_BYTES = 60_000_000


def legendre_seven(points):
    previous = points * 0.0 + 1.0
    current = points * 1.0
    for degree_index in range(1, 7):
        following = ((2 * degree_index + 1) * points * current - degree_index * previous) / (
            degree_index + 1
        )
        previous, current = (current, following)
    return current


def derivative_rows():
    degree = 7
    points = np.array([-1.0] + LOBATTO_INNER + [1.0])
    values = legendre_seven(points)
    differ = points[:, None] - points[None, :] + np.eye(degree + 1)
    matrix = values[:, None] / values[None, :] / differ
    matrix = matrix * (1.0 - np.eye(degree + 1))
    matrix[0, 0] = -degree * (degree + 1) / 4.0
    matrix[degree, degree] = degree * (degree + 1) / 4.0
    twice = 2.0 * matrix
    half = np.arange(128) // 64
    along = np.zeros((4, 4, 2, 128))
    for t in range(4):
        for source in range(4):
            along[t, source, 0] = twice[2 * t + half, 2 * source + half]
            along[t, source, 1] = twice[2 * t + half, 2 * source + 1 - half]
    rows = np.stack([np.tile(np.repeat(twice.T, 8, axis=1), 2), np.tile(twice.T, 16)]).astype(np.float32)
    high = rows.astype(BF16)
    low = (rows - high.astype(np.float32)).astype(BF16)
    parts = [along.reshape(32, 128), *high, *low]
    return np.concatenate([part.astype(np.float32) for part in parts])


def along_slope(x, rows_ref):
    turned = [pltpu.roll(value, 64, 1) for value in x]
    slopes = []
    for t in range(4):
        slope = None
        for s in range(4):
            n = 8 * t + 2 * s
            term = rows_ref[n : n + 1, :] * x[s] + rows_ref[n + 1 : n + 2, :] * turned[s]
            slope = term if slope is None else slope + term
        slopes.append(slope)
    return slopes


def fill_table(rows_ref, table):
    lane = lanes((16, 128))
    sub = lax.broadcasted_iota(jnp.int32, (16, 128), 0)
    zero = jnp.zeros((16, 128), F32)
    table[...] = jnp.zeros((2, 512, 256), BF16)
    for h in range(2):
        base = 32 + 16 * h
        row = rows_ref[base + 8 : base + 16, :]
        vertical = jnp.concatenate([row, row], axis=0)
        for g in range(16):
            here = tile(g // 8)
            j = base + 2 * g % 8
            row = jnp.where(sub >= 8, rows_ref[j + 1 : j + 2, :], rows_ref[j : j + 1, :])
            inside = ((lane >> 6) == g // 4 % 2) & ((lane & 7) == (sub & 7))
            table[h, 16 * g : 16 * g + 16, here] = jnp.where(inside, row, zero).astype(BF16)
            inside = (lane >> 3) == (sub >> 3) + 2 * (g % 8)
            table[h, 256 + 16 * g : 272 + 16 * g, here] = jnp.where(inside, vertical, zero).astype(BF16)


def split(x):
    high = x.astype(BF16)
    return high, (x - high.astype(F32)).astype(BF16)


def product(high, low, table_high, table_low):
    def dot(a, b):
        return jnp.dot(a, b, preferred_element_type=F32)

    return dot(high, table_high) + (dot(low, table_high) + dot(high, table_low))


def lanes(shape):
    return lax.broadcasted_iota(jnp.int32, shape, len(shape) - 1)


def tile(t):
    return slice(128 * t, 128 * t + 128)


def is_even(axis):
    return (lax.axis_index(axis) & 1) == 0


def holder_kernel(
    slot_hbm, store_hbm, rows_hbm,
    out_hbm,
    slot_ref, store_ref, rows_ref, table, stage, high, low, total, sems,
):
    pieces = [
        (slot_hbm, slot_ref),
        (store_hbm, store_ref),
        (rows_hbm, rows_ref),
    ]
    copies = [pltpu.make_async_copy(src, dst, sems.at[n]) for n, (src, dst) in enumerate(pieces)]
    for copy in copies:
        copy.start()
    copies[2].wait()
    fill_table(rows_ref, table)
    copies[0].wait()
    copies[1].wait()

    for g in range(16):
        rows = slice(16 * g, 16 * g + 16)
        for m in range(4):
            slot = slot_ref[2 * PEER_ORDER[2 * g + m // 2] + m % 2]
            for f in range(3):
                stage[f, g, 4 * m : 4 * m + 4, :] = store_ref[slot, f]
        slopes = along_slope([stage[0, g, :, tile(t)] for t in range(4)], rows_ref)
        for t in range(4):
            total[slice(2 * g, 2 * g + 2), :, tile(t)] = slopes[t].reshape(2, 8, 128)
        for f in range(2):
            high[f, rows], low[f, rows] = split(stage[f + 1, g])
    writes = []
    for c in range(2):
        part = slice(256 * c, 256 * c + 256)
        spread = product(high[0, :, part], low[0, :, part], table[0, 0:256], table[1, 0:256])
        spread += product(high[1, :, part], low[1, :, part], table[0, 256:512], table[1, 256:512])
        total[:, :, part] += spread.reshape(32, 8, 256)
        writes.append(
            pltpu.make_async_copy(total.at[:, :, part], out_hbm.at[:, :, part], sems.at[3 + c])
        )
        writes[c].start()
    for write in writes:
        write.wait()


def trace_kernel(adj_ref, along_one, along_two, cross_one, cross_two):
    even = is_even("along")
    for f in range(4):
        for c in range(4):
            rows = slice(4 * c, 4 * c + 4)
            first = adj_ref[f, 0, c, :, tile(0)]
            last = adj_ref[f, 7, c, :, tile(3)]
            along_one[f, rows, :] = jnp.where(even, last, first)
            along_two[f, rows, :] = jnp.where(even, first, last)
    even = is_even("cross")
    j = (lanes((4, 128)) >> 3) & 7
    for f in range(4):
        for t in range(4):
            last = pltpu.roll(adj_ref[f, 0, 3, :, tile(t)], 72, 1)
            first = adj_ref[f, 0, 0, :, tile(t)]
            for a in range(1, 8):
                other = adj_ref[f, a, 3, :, tile(t)]
                last = jnp.where(j == a, pltpu.roll(other, (72 + 8 * a) % 128, 1), last)
                other = adj_ref[f, a, 0, :, tile(t)]
                first = jnp.where(j == a, pltpu.roll(other, 8 * a, 1), first)
            cross_one[f, :, tile(t)] = jnp.where(even, last, first)
            cross_two[f, :, tile(t)] = jnp.where(even, first, last)


def volume_kernel(
    node_ref, residual_ref, adj_ref, rows_ref, out_ref, table, state, high, low, slope_x, slope_y, slope_z, ground
):
    fill_table(rows_ref, table)
    row = {2: 0, 0: 128, 3: 256}
    state[:, 0] = jnp.zeros((4, 16, 512), F32)
    state[:, 9] = jnp.zeros((4, 16, 512), F32)

    def load(a, carry):
        for f in range(4):
            for c in range(4):
                state[f, a + 1, 4 * c : 4 * c + 4, :] = adj_ref[f, a, c]
            slopes = along_slope([state[f, a + 1, :, tile(t)] for t in range(4)], rows_ref)
            for t in range(4):
                slope_x[f, a, :, tile(t)] = slopes[t]
            if f in row:
                rows = pl.ds(pl.multiple_of(row[f] + a * 16, 16), 16)
                high[rows], low[rows] = split(state[f, a + 1])
        return carry

    lax.fori_loop(0, 8, load, 0, unroll=8)
    for c in range(2):
        part = slice(256 * c, 256 * c + 256)
        slope_y[:, part] = product(high[0:256, part], low[0:256, part], table[0, 0:256], table[1, 0:256])
        slope_z[:, part] = product(
            high[128:384, part], low[128:384, part], table[0, 256:512], table[1, 256:512]
        )

    node = node_ref[...]
    residual = residual_ref[...]
    target = lax.broadcasted_iota(jnp.int32, (128, 128), 0)
    spread = jnp.where(target == 4 * (node >> 6), residual, 0.0)
    place = lax.broadcasted_iota(jnp.int32, (512, 128), 0) == 8 * (node & 63)
    place = jnp.where(place, 1.0, 0.0).astype(BF16)
    ones, rest = split(spread)
    twos = (spread - ones.astype(F32) - rest.astype(F32)).astype(BF16)

    def match(a):
        return lax.dot_general(a, place, (((1,), (1,)), ((), ())), preferred_element_type=F32)

    ground[...] = match(ones) + (match(rest) + match(twos))

    lane = lanes((8, 128))
    sub = lax.broadcasted_iota(jnp.int32, (8, 128), 0)
    j = (lane >> 3) & 7
    k = lane & 7
    e = sub & 3
    odd = sub >= 4
    top_y = j == 7
    top_z = k == 7
    floor = e == 0
    ceiling = e == 3
    zero = jnp.zeros((8, 128), F32)
    sign_y = jnp.where(j == 0, HALF_LIFT, jnp.where(top_y, -HALF_LIFT, 0.0))
    size_y = jnp.where((j == 0) | top_y, -HALF_LIFT * ALPHA, 0.0)
    sign_z = jnp.where(k == 0, HALF_LIFT, jnp.where(top_z, -HALF_LIFT, 0.0))
    size_z = jnp.where((k == 0) | top_z, -HALF_LIFT * ALPHA, 0.0)

    def step(a, carry):
        for t in range(4):
            here = tile(t)
            q = [[state[f, a + 1, 8 * g : 8 * g + 8, here] for g in range(2)] for f in range(4)]
            dy = [[None] * 2 for _ in range(4)]
            dz = [[None] * 2 for _ in range(4)]
            dx = [[None] * 2 for _ in range(4)]
            for f in range(4):
                swap = [pltpu.roll(q[f][g], 4, 0) for g in range(2)]
                before = [jnp.where(odd, swap[0], zero), jnp.where(odd, swap[1], swap[0])]
                after = [jnp.where(odd, swap[1], swap[0]), jnp.where(odd, zero, swap[1])]
                for g in range(2):
                    x = q[f][g]
                    outer = jnp.where(top_y, pltpu.roll(after[g], 56, 1), pltpu.roll(before[g], 72, 1))
                    dy[f][g] = x - outer
                    below = pltpu.roll(pltpu.roll(x, 1, 0), 121, 1)
                    below = jnp.where(floor, -x if f == 3 else x, below)
                    above = pltpu.roll(pltpu.roll(x, 7, 0), 7, 1)
                    above = jnp.where(ceiling, zero, above)
                    dz[f][g] = x - jnp.where(top_z, above, below)
                    if t == 0:
                        outer = pltpu.roll(state[f, a, 8 * g : 8 * g + 8, tile(3)], 64, 1)
                        dx[f][g] = jnp.where(lane < 64, x - outer, zero)
                    if t == 3:
                        outer = pltpu.roll(state[f, a + 2, 8 * g : 8 * g + 8, tile(0)], 64, 1)
                        dx[f][g] = jnp.where(lane >= 64, x - outer, zero)
            for g in range(2):
                def rows(f, base=0):
                    return pl.ds(pl.multiple_of(row[f] - base + a * 16 + 8 * g, 8), 8)

                gx = [slope_x[f, a, 8 * g : 8 * g + 8, here] for f in range(4)]
                gy = {f: slope_y[rows(f), here] for f in (2, 0)}
                gz = {f: slope_z[rows(f, 128), here] for f in (0, 3)}
                rate = [
                    MACH * gx[0] + gx[1] + gy[2] + gz[3],
                    MACH * gx[1] + gx[0],
                    MACH * gx[2] + gy[0],
                    MACH * gx[3] + gz[0],
                ]
                for f in range(4):
                    rate[f] = rate[f] + size_y * dy[f][g] + size_z * dz[f][g]
                rate[0] = rate[0] + sign_y * dy[2][g] + sign_z * dz[3][g]
                rate[2] = rate[2] + sign_y * dy[0][g]
                rate[3] = rate[3] + sign_z * dz[0][g]
                if t in (0, 3):
                    s = -1.0 if t == 0 else 1.0
                    d = [dx[f][g] for f in range(4)]
                    own = -HALF_LIFT * (s * MACH + ALPHA)
                    rate[0] = rate[0] + own * d[0] - (HALF_LIFT * s) * d[1]
                    rate[1] = rate[1] + own * d[1] - (HALF_LIFT * s) * d[0]
                    rate[2] = rate[2] + own * d[2]
                    rate[3] = rate[3] + own * d[3]
                new = [q[f][g] + TIME_STEP * rate[f] for f in range(4)]
                source = ground[pl.ds(pl.multiple_of(a * 16 + 8 * g, 8), 8), here]
                new[0] = new[0] + (TIME_STEP * SOURCE_GAIN) * source
                for f in range(4):
                    out_ref[f, a, 8 * g : 8 * g + 8, here] = new[f]
        return carry

    lax.fori_loop(0, 8, step, 0, unroll=8)


def finish_kernel(
    arrival_ref, adj_ref, new_ref, cross_two, along_two, cross_one, along_one, received_ref,
    next_hbm, kappa_hbm, next_ref, kappa_ref, edge, side, place, sems,
):
    for n, peer in enumerate(PEER_ORDER):
        place[peer] = n
    lift = TIME_STEP * HALF_LIFT
    lane = lanes((4, 128))
    j = (lane >> 3) & 7

    def arrived(axis, one, two, s, f, index):
        use_one = is_even(axis) if s > 0 else jnp.logical_not(is_even(axis))
        return jnp.where(use_one, one[(f, *index)], two[(f, *index)])

    def along_terms(s, rows):
        q = [arrived("along", along_one, along_two, s, f, (rows, slice(None))) for f in range(4)]
        q = [pltpu.roll(x, 64, 1) for x in q]
        own = lift * (s * MACH + ALPHA)
        return [own * q[0] + (lift * s) * q[1], own * q[1] + (lift * s) * q[0], own * q[2], own * q[3]]

    def cross_terms(s, t):
        q = [arrived("cross", cross_one, cross_two, s, f, (slice(None), tile(t))) for f in range(4)]
        own = lift * ALPHA
        return [
            own * q[0] + (lift * s) * q[2], own * q[1], own * q[2] + (lift * s) * q[0], own * q[3],
        ]

    for c in range(4):
        rows = slice(4 * c, 4 * c + 4)
        low = along_terms(-1.0, rows)
        high = along_terms(1.0, rows)
        for f in range(4):
            edge[0, f, rows, :] = jnp.where(lane < 64, low[f], 0.0)
            edge[1, f, rows, :] = jnp.where(lane >= 64, high[f], 0.0)
    for t in range(4):
        low = cross_terms(-1.0, t)
        high = cross_terms(1.0, t)
        for f in range(4):
            side[0, f, :, tile(t)] = low[f]
            side[1, f, :, tile(t)] = high[f]
    writes = []
    for f in range(4):
        for t in range(4):
            for a in range(8):
                for c in range(4):
                    value = new_ref[f, a, 4 * c : 4 * c + 4, tile(t)]
                    if c == 0:
                        beyond = pltpu.roll(side[0, f, :, tile(t)], (128 - 8 * a) % 128, 1)
                        value = value + jnp.where(j == 0, beyond, 0.0)
                    if c == 3:
                        beyond = pltpu.roll(side[1, f, :, tile(t)], (56 - 8 * a) % 128, 1)
                        value = value + jnp.where(j == 7, beyond, 0.0)
                    if t == 0 and a == 0:
                        value = value + edge[0, f, 4 * c : 4 * c + 4, :]
                    if t == 3 and a == 7:
                        value = value + edge[1, f, 4 * c : 4 * c + 4, :]
                    next_ref[f, a, c, :, tile(t)] = value
        writes.append(pltpu.make_async_copy(next_ref.at[f], next_hbm.at[f], sems.at[f]))
        writes[f].start()
    for a in range(8):
        for c in range(4):
            q = arrival_ref[a, c]
            clipped = jnp.maximum(q, 0)
            holder = place[clipped >> 1]
            second = (clipped & 1) == 1
            block = jnp.where(second, received_ref[holder, 4:8, :], received_ref[holder, 0:4, :])
            value = TIME_STEP * adj_ref[0, a, c] * block
            kappa_ref[a, c] = jnp.where(q >= 0, value, 0.0)
    writes.append(pltpu.make_async_copy(kappa_ref, kappa_hbm, sems.at[4]))
    writes[4].start()
    for write in writes:
        write.wait()


VMEM = pl.BlockSpec(memory_space=pltpu.VMEM)
HBM = pl.BlockSpec(memory_space=pltpu.HBM)
SMEM = pl.BlockSpec(memory_space=pltpu.SMEM)


def kernel(body, out_shape, in_specs, scratch, flops, moved, out_specs=None, limit=VMEM_BYTES):
    return pl.pallas_call(
        body,
        out_shape=out_shape,
        in_specs=in_specs,
        out_specs=out_specs or jax.tree.map(lambda _: VMEM, out_shape),
        scratch_shapes=scratch,
        compiler_params=pltpu.CompilerParams(vmem_limit_bytes=limit),
        cost_estimate=pl.CostEstimate(flops=flops, bytes_accessed=moved, transcendentals=0),
    )


def array(*shape):
    return jax.ShapeDtypeStruct(shape, F32)


def exchange(value, axis, start):
    pairs = []
    for i in range(start, lax.axis_size(axis) - 1, 2):
        pairs += [(i, i + 1), (i + 1, i)]
    return lax.ppermute(value, axis, pairs)


def per_device(adjoint_state, snapshot_store, dispatch_slot, arrival_slot, mic_node, mic_residual):
    rows = jnp.asarray(derivative_rows())
    outgoing = kernel(
        holder_kernel,
        array(32, 8, 512),
        [HBM] * 3,
        [
            pltpu.SMEM((64,), jnp.int32),
            pltpu.VMEM((64, 3, 4, 512), F32),
            pltpu.VMEM((64, 128), F32),
            pltpu.VMEM((2, 512, 256), BF16),
            pltpu.VMEM((3, 16, 16, 512), F32),
            pltpu.VMEM((2, 256, 512), BF16),
            pltpu.VMEM((2, 256, 512), BF16),
            pltpu.VMEM((32, 8, 512), F32),
            pltpu.SemaphoreType.DMA((5,)),
        ],
        3_000_000_000, 5_000_000,
        HBM,
        HOLDER_BYTES,
    )(dispatch_slot, snapshot_store, rows)
    received = lax.all_to_all(
        outgoing, "cross", split_axis=0, concat_axis=0, axis_index_groups=[list(PEER_ORDER)], tiled=True
    )
    along_one, along_two, cross_one, cross_two = kernel(
        trace_kernel,
        (array(4, 16, 128), array(4, 16, 128), array(4, 4, 512), array(4, 4, 512)),
        [VMEM],
        [],
        1_000_000, 500_000,
    )(adjoint_state)
    updated = kernel(
        volume_kernel,
        array(4, 8, 16, 512),
        [VMEM] * 4,
        [
            pltpu.VMEM((2, 512, 256), BF16),
            pltpu.VMEM((4, 10, 16, 512), F32),
            pltpu.VMEM((384, 512), BF16),
            pltpu.VMEM((384, 512), BF16),
            pltpu.VMEM((4, 8, 16, 512), F32),
            pltpu.VMEM((256, 512), F32),
            pltpu.VMEM((256, 512), F32),
            pltpu.VMEM((128, 512), F32),
        ],
        4_000_000_000, 4_000_000,
    )(mic_node.reshape(1, 128), mic_residual.reshape(1, 128), adjoint_state, rows)
    along_one = exchange(along_one, "along", 0)
    along_two = exchange(along_two, "along", 1)
    cross_one = exchange(cross_one, "cross", 0)
    cross_two = exchange(cross_two, "cross", 1)
    return kernel(
        finish_kernel,
        (array(4, 8, 4, 4, 512), array(8, 4, 4, 512)),
        [SMEM] + [VMEM] * 7,
        [
            pltpu.VMEM((4, 8, 4, 4, 512), F32),
            pltpu.VMEM((8, 4, 4, 512), F32),
            pltpu.VMEM((2, 4, 16, 128), F32),
            pltpu.VMEM((2, 4, 4, 512), F32),
            pltpu.SMEM((32,), jnp.int32),
            pltpu.SemaphoreType.DMA((5,)),
        ],
        10_000_000, 4_000_000,
        (HBM, HBM),
    )(
        arrival_slot, adjoint_state, updated, cross_two, along_two, cross_one, along_one, received
    )


def solution(mesh):
    in_specs = (
        P(None, "along", "cross", None, None),
        P(("along", "cross"), None, None, None),
        P(("along", "cross")),
        P("along", "cross"),
        P(("along", "cross")),
        P(("along", "cross")),
    )
    out_specs = (P(None, "along", "cross", None, None), P("along", "cross", None, None))
    return jax.shard_map(
        per_device, mesh=mesh, in_specs=in_specs, out_specs=out_specs, check_vma=False
    )
```

```python
import jax
import jax.numpy as jnp
import numpy as np
from jax import lax
from jax.experimental import pallas as pl
from jax.experimental.pallas import tpu as pltpu
from jax.sharding import PartitionSpec as P

MACH = 0.3
ALPHA = 1.3
LIFT_SCALE = 56.0
TIME_STEP = 0.004
SOURCE_GAIN = 50.0
HALF_LIFT = 0.5 * LIFT_SCALE
LOBATTO_INNER = [
    -0.8717401485096066,
    -0.5917001814331423,
    -0.2092992179024789,
    0.2092992179024789,
    0.5917001814331423,
    0.8717401485096066,
]
F32 = jnp.float32
BF16 = jnp.bfloat16
VMEM_BYTES = 24 * 1024 * 1024
PEER_ORDER = (31, 23, 28, 26, 12, 21, 8, 19, 18, 3, 2, 1, 24, 4, 14, 11, 17, 0, 7, 27, 22, 5, 16, 25, 6, 15, 9, 10, 30, 29, 13, 20)
HOLDER_BYTES = 60_000_000


def legendre_seven(points):
    previous = points * 0.0 + 1.0
    current = points * 1.0
    for degree_index in range(1, 7):
        following = ((2 * degree_index + 1) * points * current - degree_index * previous) / (
            degree_index + 1
        )
        previous, current = (current, following)
    return current


def derivative_rows():
    degree = 7
    points = np.array([-1.0] + LOBATTO_INNER + [1.0])
    values = legendre_seven(points)
    differ = points[:, None] - points[None, :] + np.eye(degree + 1)
    matrix = values[:, None] / values[None, :] / differ
    matrix = matrix * (1.0 - np.eye(degree + 1))
    matrix[0, 0] = -degree * (degree + 1) / 4.0
    matrix[degree, degree] = degree * (degree + 1) / 4.0
    twice = 2.0 * matrix
    half = np.arange(128) // 64
    along = np.zeros((4, 4, 2, 128))
    for t in range(4):
        for source in range(4):
            along[t, source, 0] = twice[2 * t + half, 2 * source + half]
            along[t, source, 1] = twice[2 * t + half, 2 * source + 1 - half]
    rows = np.stack([np.tile(np.repeat(twice.T, 8, axis=1), 2), np.tile(twice.T, 16)]).astype(np.float32)
    high = rows.astype(BF16)
    low = (rows - high.astype(np.float32)).astype(BF16)
    parts = [along.reshape(32, 128), *high, *low]
    return np.concatenate([part.astype(np.float32) for part in parts])


def along_slope(x, rows_ref):
    turned = [pltpu.roll(value, 64, 1) for value in x]
    slopes = []
    for t in range(4):
        slope = None
        for s in range(4):
            n = 8 * t + 2 * s
            term = rows_ref[n : n + 1, :] * x[s] + rows_ref[n + 1 : n + 2, :] * turned[s]
            slope = term if slope is None else slope + term
        slopes.append(slope)
    return slopes


def fill_table(rows_ref, table):
    lane = lanes((16, 128))
    sub = lax.broadcasted_iota(jnp.int32, (16, 128), 0)
    zero = jnp.zeros((16, 128), F32)
    table[...] = jnp.zeros((2, 512, 256), BF16)
    for h in range(2):
        base = 32 + 16 * h
        row = rows_ref[base + 8 : base + 16, :]
        vertical = jnp.concatenate([row, row], axis=0)
        for g in range(16):
            here = tile(g // 8)
            j = base + 2 * g % 8
            row = jnp.where(sub >= 8, rows_ref[j + 1 : j + 2, :], rows_ref[j : j + 1, :])
            inside = ((lane >> 6) == g // 4 % 2) & ((lane & 7) == (sub & 7))
            table[h, 16 * g : 16 * g + 16, here] = jnp.where(inside, row, zero).astype(BF16)
            inside = (lane >> 3) == (sub >> 3) + 2 * (g % 8)
            table[h, 256 + 16 * g : 272 + 16 * g, here] = jnp.where(inside, vertical, zero).astype(BF16)


def split(x):
    high = x.astype(BF16)
    return high, (x - high.astype(F32)).astype(BF16)


def product(high, low, table_high, table_low):
    def dot(a, b):
        return jnp.dot(a, b, preferred_element_type=F32)

    return dot(high, table_high) + (dot(low, table_high) + dot(high, table_low))


def lanes(shape):
    return lax.broadcasted_iota(jnp.int32, shape, len(shape) - 1)


def tile(t):
    return slice(128 * t, 128 * t + 128)


def is_even(axis):
    return (lax.axis_index(axis) & 1) == 0


def holder_kernel(
    slot_hbm, store_hbm, rows_hbm,
    out_hbm,
    slot_ref, store_ref, rows_ref, table, stage, high, low, total, sems,
):
    pieces = [
        (slot_hbm, slot_ref),
        (store_hbm, store_ref),
        (rows_hbm, rows_ref),
    ]
    copies = [pltpu.make_async_copy(src, dst, sems.at[n]) for n, (src, dst) in enumerate(pieces)]
    for copy in copies:
        copy.start()
    copies[2].wait()
    fill_table(rows_ref, table)
    copies[0].wait()
    copies[1].wait()

    for g in range(16):
        rows = slice(16 * g, 16 * g + 16)
        for m in range(4):
            slot = slot_ref[2 * PEER_ORDER[2 * g + m // 2] + m % 2]
            for f in range(3):
                stage[f, g, 4 * m : 4 * m + 4, :] = store_ref[slot, f]
        slopes = along_slope([stage[0, g, :, tile(t)] for t in range(4)], rows_ref)
        for t in range(4):
            total[slice(2 * g, 2 * g + 2), :, tile(t)] = slopes[t].reshape(2, 8, 128)
        for f in range(2):
            high[f, rows], low[f, rows] = split(stage[f + 1, g])
    writes = []
    for c in range(2):
        part = slice(256 * c, 256 * c + 256)
        spread = product(high[0, :, part], low[0, :, part], table[0, 0:256], table[1, 0:256])
        spread += product(high[1, :, part], low[1, :, part], table[0, 256:512], table[1, 256:512])
        total[:, :, part] += spread.reshape(32, 8, 256)
        writes.append(
            pltpu.make_async_copy(total.at[:, :, part], out_hbm.at[:, :, part], sems.at[3 + c])
        )
        writes[c].start()
    for write in writes:
        write.wait()


def trace_kernel(adj_ref, along_one, along_two, cross_one, cross_two):
    even = is_even("along")
    for f in range(4):
        for c in range(4):
            rows = slice(4 * c, 4 * c + 4)
            first = adj_ref[f, 0, c, :, tile(0)]
            last = adj_ref[f, 7, c, :, tile(3)]
            along_one[f, rows, :] = jnp.where(even, last, first)
            along_two[f, rows, :] = jnp.where(even, first, last)
    even = is_even("cross")
    j = (lanes((4, 128)) >> 3) & 7
    for f in range(4):
        for t in range(4):
            last = pltpu.roll(adj_ref[f, 0, 3, :, tile(t)], 72, 1)
            first = adj_ref[f, 0, 0, :, tile(t)]
            for a in range(1, 8):
                other = adj_ref[f, a, 3, :, tile(t)]
                last = jnp.where(j == a, pltpu.roll(other, (72 + 8 * a) % 128, 1), last)
                other = adj_ref[f, a, 0, :, tile(t)]
                first = jnp.where(j == a, pltpu.roll(other, 8 * a, 1), first)
            cross_one[f, :, tile(t)] = jnp.where(even, last, first)
            cross_two[f, :, tile(t)] = jnp.where(even, first, last)


def volume_kernel(
    node_ref, residual_ref, adj_ref, rows_ref, out_ref, table, state, high, low, slope_x, slope_y, slope_z, ground
):
    fill_table(rows_ref, table)
    row = {2: 0, 0: 128, 3: 256}
    state[:, 0] = jnp.zeros((4, 16, 512), F32)
    state[:, 9] = jnp.zeros((4, 16, 512), F32)

    def load(a, carry):
        for f in range(4):
            for c in range(4):
                state[f, a + 1, 4 * c : 4 * c + 4, :] = adj_ref[f, a, c]
            slopes = along_slope([state[f, a + 1, :, tile(t)] for t in range(4)], rows_ref)
            for t in range(4):
                slope_x[f, a, :, tile(t)] = slopes[t]
            if f in row:
                rows = pl.ds(pl.multiple_of(row[f] + a * 16, 16), 16)
                high[rows], low[rows] = split(state[f, a + 1])
        return carry

    lax.fori_loop(0, 8, load, 0, unroll=8)
    for c in range(2):
        part = slice(256 * c, 256 * c + 256)
        slope_y[:, part] = product(high[0:256, part], low[0:256, part], table[0, 0:256], table[1, 0:256])
        slope_z[:, part] = product(
            high[128:384, part], low[128:384, part], table[0, 256:512], table[1, 256:512]
        )

    node = node_ref[...]
    residual = residual_ref[...]
    target = lax.broadcasted_iota(jnp.int32, (128, 128), 0)
    spread = jnp.where(target == 4 * (node >> 6), residual, 0.0)
    place = lax.broadcasted_iota(jnp.int32, (512, 128), 0) == 8 * (node & 63)
    place = jnp.where(place, 1.0, 0.0).astype(BF16)
    ones, rest = split(spread)
    twos = (spread - ones.astype(F32) - rest.astype(F32)).astype(BF16)

    def match(a):
        return lax.dot_general(a, place, (((1,), (1,)), ((), ())), preferred_element_type=F32)

    ground[...] = match(ones) + (match(rest) + match(twos))

    lane = lanes((8, 128))
    sub = lax.broadcasted_iota(jnp.int32, (8, 128), 0)
    j = (lane >> 3) & 7
    k = lane & 7
    e = sub & 3
    odd = sub >= 4
    top_y = j == 7
    top_z = k == 7
    floor = e == 0
    ceiling = e == 3
    zero = jnp.zeros((8, 128), F32)
    sign_y = jnp.where(j == 0, HALF_LIFT, jnp.where(top_y, -HALF_LIFT, 0.0))
    size_y = jnp.where((j == 0) | top_y, -HALF_LIFT * ALPHA, 0.0)
    sign_z = jnp.where(k == 0, HALF_LIFT, jnp.where(top_z, -HALF_LIFT, 0.0))
    size_z = jnp.where((k == 0) | top_z, -HALF_LIFT * ALPHA, 0.0)

    def step(a, carry):
        for t in range(4):
            here = tile(t)
            q = [[state[f, a + 1, 8 * g : 8 * g + 8, here] for g in range(2)] for f in range(4)]
            dy = [[None] * 2 for _ in range(4)]
            dz = [[None] * 2 for _ in range(4)]
            dx = [[None] * 2 for _ in range(4)]
            for f in range(4):
                swap = [pltpu.roll(q[f][g], 4, 0) for g in range(2)]
                before = [jnp.where(odd, swap[0], zero), jnp.where(odd, swap[1], swap[0])]
                after = [jnp.where(odd, swap[1], swap[0]), jnp.where(odd, zero, swap[1])]
                for g in range(2):
                    x = q[f][g]
                    outer = jnp.where(top_y, pltpu.roll(after[g], 56, 1), pltpu.roll(before[g], 72, 1))
                    dy[f][g] = x - outer
                    below = pltpu.roll(pltpu.roll(x, 1, 0), 121, 1)
                    below = jnp.where(floor, -x if f == 3 else x, below)
                    above = pltpu.roll(pltpu.roll(x, 7, 0), 7, 1)
                    above = jnp.where(ceiling, zero, above)
                    dz[f][g] = x - jnp.where(top_z, above, below)
                    if t == 0:
                        outer = pltpu.roll(state[f, a, 8 * g : 8 * g + 8, tile(3)], 64, 1)
                        dx[f][g] = jnp.where(lane < 64, x - outer, zero)
                    if t == 3:
                        outer = pltpu.roll(state[f, a + 2, 8 * g : 8 * g + 8, tile(0)], 64, 1)
                        dx[f][g] = jnp.where(lane >= 64, x - outer, zero)
            for g in range(2):
                def rows(f, base=0):
                    return pl.ds(pl.multiple_of(row[f] - base + a * 16 + 8 * g, 8), 8)

                gx = [slope_x[f, a, 8 * g : 8 * g + 8, here] for f in range(4)]
                gy = {f: slope_y[rows(f), here] for f in (2, 0)}
                gz = {f: slope_z[rows(f, 128), here] for f in (0, 3)}
                rate = [
                    MACH * gx[0] + gx[1] + gy[2] + gz[3],
                    MACH * gx[1] + gx[0],
                    MACH * gx[2] + gy[0],
                    MACH * gx[3] + gz[0],
                ]
                for f in range(4):
                    rate[f] = rate[f] + size_y * dy[f][g] + size_z * dz[f][g]
                rate[0] = rate[0] + sign_y * dy[2][g] + sign_z * dz[3][g]
                rate[2] = rate[2] + sign_y * dy[0][g]
                rate[3] = rate[3] + sign_z * dz[0][g]
                if t in (0, 3):
                    s = -1.0 if t == 0 else 1.0
                    d = [dx[f][g] for f in range(4)]
                    own = -HALF_LIFT * (s * MACH + ALPHA)
                    rate[0] = rate[0] + own * d[0] - (HALF_LIFT * s) * d[1]
                    rate[1] = rate[1] + own * d[1] - (HALF_LIFT * s) * d[0]
                    rate[2] = rate[2] + own * d[2]
                    rate[3] = rate[3] + own * d[3]
                new = [q[f][g] + TIME_STEP * rate[f] for f in range(4)]
                source = ground[pl.ds(pl.multiple_of(a * 16 + 8 * g, 8), 8), here]
                new[0] = new[0] + (TIME_STEP * SOURCE_GAIN) * source
                for f in range(4):
                    out_ref[f, a, 8 * g : 8 * g + 8, here] = new[f]
        return carry

    lax.fori_loop(0, 8, step, 0, unroll=8)


def finish_kernel(
    arrival_ref, adj_ref, new_ref, cross_two, along_two, cross_one, along_one, received_ref,
    next_hbm, kappa_hbm, next_ref, kappa_ref, edge, side, place, sems,
):
    for n, peer in enumerate(PEER_ORDER):
        place[peer] = n
    lift = TIME_STEP * HALF_LIFT
    lane = lanes((4, 128))
    j = (lane >> 3) & 7

    def arrived(axis, one, two, s, f, index):
        use_one = is_even(axis) if s > 0 else jnp.logical_not(is_even(axis))
        return jnp.where(use_one, one[(f, *index)], two[(f, *index)])

    def along_terms(s, rows):
        q = [arrived("along", along_one, along_two, s, f, (rows, slice(None))) for f in range(4)]
        q = [pltpu.roll(x, 64, 1) for x in q]
        own = lift * (s * MACH + ALPHA)
        return [own * q[0] + (lift * s) * q[1], own * q[1] + (lift * s) * q[0], own * q[2], own * q[3]]

    def cross_terms(s, t):
        q = [arrived("cross", cross_one, cross_two, s, f, (slice(None), tile(t))) for f in range(4)]
        own = lift * ALPHA
        return [
            own * q[0] + (lift * s) * q[2], own * q[1], own * q[2] + (lift * s) * q[0], own * q[3],
        ]

    for c in range(4):
        rows = slice(4 * c, 4 * c + 4)
        low = along_terms(-1.0, rows)
        high = along_terms(1.0, rows)
        for f in range(4):
            edge[0, f, rows, :] = jnp.where(lane < 64, low[f], 0.0)
            edge[1, f, rows, :] = jnp.where(lane >= 64, high[f], 0.0)
    for t in range(4):
        low = cross_terms(-1.0, t)
        high = cross_terms(1.0, t)
        for f in range(4):
            side[0, f, :, tile(t)] = low[f]
            side[1, f, :, tile(t)] = high[f]
    writes = []
    for f in range(4):
        for t in range(4):
            for a in range(8):
                for c in range(4):
                    value = new_ref[f, a, 4 * c : 4 * c + 4, tile(t)]
                    if c == 0:
                        beyond = pltpu.roll(side[0, f, :, tile(t)], (128 - 8 * a) % 128, 1)
                        value = value + jnp.where(j == 0, beyond, 0.0)
                    if c == 3:
                        beyond = pltpu.roll(side[1, f, :, tile(t)], (56 - 8 * a) % 128, 1)
                        value = value + jnp.where(j == 7, beyond, 0.0)
                    if t == 0 and a == 0:
                        value = value + edge[0, f, 4 * c : 4 * c + 4, :]
                    if t == 3 and a == 7:
                        value = value + edge[1, f, 4 * c : 4 * c + 4, :]
                    next_ref[f, a, c, :, tile(t)] = value
        writes.append(pltpu.make_async_copy(next_ref.at[f], next_hbm.at[f], sems.at[f]))
        writes[f].start()
    for a in range(8):
        for c in range(4):
            q = arrival_ref[a, c]
            clipped = jnp.maximum(q, 0)
            holder = place[clipped >> 1]
            second = (clipped & 1) == 1
            block = jnp.where(second, received_ref[holder, 4:8, :], received_ref[holder, 0:4, :])
            value = TIME_STEP * adj_ref[0, a, c] * block
            kappa_ref[a, c] = jnp.where(q >= 0, value, 0.0)
    writes.append(pltpu.make_async_copy(kappa_ref, kappa_hbm, sems.at[4]))
    writes[4].start()
    for write in writes:
        write.wait()


VMEM = pl.BlockSpec(memory_space=pltpu.VMEM)
HBM = pl.BlockSpec(memory_space=pltpu.HBM)
SMEM = pl.BlockSpec(memory_space=pltpu.SMEM)


def kernel(body, out_shape, in_specs, scratch, flops, moved, out_specs=None, limit=VMEM_BYTES):
    return pl.pallas_call(
        body,
        out_shape=out_shape,
        in_specs=in_specs,
        out_specs=out_specs or jax.tree.map(lambda _: VMEM, out_shape),
        scratch_shapes=scratch,
        compiler_params=pltpu.CompilerParams(vmem_limit_bytes=limit),
        cost_estimate=pl.CostEstimate(flops=flops, bytes_accessed=moved, transcendentals=0),
    )


def array(*shape):
    return jax.ShapeDtypeStruct(shape, F32)


def exchange(value, axis, start):
    pairs = []
    for i in range(start, lax.axis_size(axis) - 1, 2):
        pairs += [(i, i + 1), (i + 1, i)]
    return lax.ppermute(value, axis, pairs)


def per_device(adjoint_state, snapshot_store, dispatch_slot, arrival_slot, mic_node, mic_residual):
    rows = jnp.asarray(derivative_rows())
    outgoing = kernel(
        holder_kernel,
        array(32, 8, 512),
        [HBM] * 3,
        [
            pltpu.SMEM((64,), jnp.int32),
            pltpu.VMEM((64, 3, 4, 512), F32),
            pltpu.VMEM((64, 128), F32),
            pltpu.VMEM((2, 512, 256), BF16),
            pltpu.VMEM((3, 16, 16, 512), F32),
            pltpu.VMEM((2, 256, 512), BF16),
            pltpu.VMEM((2, 256, 512), BF16),
            pltpu.VMEM((32, 8, 512), F32),
            pltpu.SemaphoreType.DMA((5,)),
        ],
        3_000_000_000, 5_000_000,
        HBM,
        HOLDER_BYTES,
    )(dispatch_slot, snapshot_store, rows)
    received = lax.all_to_all(
        outgoing, "cross", split_axis=0, concat_axis=0, axis_index_groups=[list(PEER_ORDER)], tiled=True
    )
    along_one, along_two, cross_one, cross_two = kernel(
        trace_kernel,
        (array(4, 16, 128), array(4, 16, 128), array(4, 4, 512), array(4, 4, 512)),
        [VMEM],
        [],
        1_000_000, 500_000,
    )(adjoint_state)
    updated = kernel(
        volume_kernel,
        array(4, 8, 16, 512),
        [VMEM] * 4,
        [
            pltpu.VMEM((2, 512, 256), BF16),
            pltpu.VMEM((4, 10, 16, 512), F32),
            pltpu.VMEM((384, 512), BF16),
            pltpu.VMEM((384, 512), BF16),
            pltpu.VMEM((4, 8, 16, 512), F32),
            pltpu.VMEM((256, 512), F32),
            pltpu.VMEM((256, 512), F32),
            pltpu.VMEM((128, 512), F32),
        ],
        4_000_000_000, 4_000_000,
    )(mic_node.reshape(1, 128), mic_residual.reshape(1, 128), adjoint_state, rows)
    along_one = exchange(along_one, "along", 0)
    along_two = exchange(along_two, "along", 1)
    cross_one = exchange(cross_one, "cross", 0)
    cross_two = exchange(cross_two, "cross", 1)
    return kernel(
        finish_kernel,
        (array(4, 8, 4, 4, 512), array(8, 4, 4, 512)),
        [SMEM] + [VMEM] * 7,
        [
            pltpu.VMEM((4, 8, 4, 4, 512), F32),
            pltpu.VMEM((8, 4, 4, 512), F32),
            pltpu.VMEM((2, 4, 16, 128), F32),
            pltpu.VMEM((2, 4, 4, 512), F32),
            pltpu.SMEM((32,), jnp.int32),
            pltpu.SemaphoreType.DMA((5,)),
        ],
        10_000_000, 4_000_000,
        (HBM, HBM),
    )(
        arrival_slot, adjoint_state, updated, cross_two, along_two, cross_one, along_one, received
    )


def solution(mesh):
    in_specs = (
        P(None, "along", "cross", None, None),
        P(("along", "cross"), None, None, None),
        P(("along", "cross")),
        P("along", "cross"),
        P(("along", "cross")),
        P(("along", "cross")),
    )
    out_specs = (P(None, "along", "cross", None, None), P("along", "cross", None, None))
    return jax.shard_map(
        per_device, mesh=mesh, in_specs=in_specs, out_specs=out_specs, check_vma=False
    )
```

```python
import jax
import jax.numpy as jnp
import numpy as np
from jax import lax
from jax.experimental import pallas as pl
from jax.experimental.pallas import tpu as pltpu
from jax.sharding import PartitionSpec as P

MACH = 0.3
ALPHA = 1.3
LIFT_SCALE = 56.0
TIME_STEP = 0.004
SOURCE_GAIN = 50.0
HALF_LIFT = 0.5 * LIFT_SCALE
LOBATTO_INNER = [
    -0.8717401485096066,
    -0.5917001814331423,
    -0.2092992179024789,
    0.2092992179024789,
    0.5917001814331423,
    0.8717401485096066,
]
F32 = jnp.float32
BF16 = jnp.bfloat16
VMEM_BYTES = 24 * 1024 * 1024
PEER_ORDER = (31, 23, 28, 26, 12, 21, 8, 19, 18, 3, 2, 1, 24, 4, 14, 11, 17, 0, 7, 27, 22, 5, 16, 25, 6, 15, 9, 10, 30, 29, 13, 20)
HOLDER_BYTES = 60_000_000


def legendre_seven(points):
    previous = points * 0.0 + 1.0
    current = points * 1.0
    for degree_index in range(1, 7):
        following = ((2 * degree_index + 1) * points * current - degree_index * previous) / (
            degree_index + 1
        )
        previous, current = (current, following)
    return current


def derivative_rows():
    degree = 7
    points = np.array([-1.0] + LOBATTO_INNER + [1.0])
    values = legendre_seven(points)
    differ = points[:, None] - points[None, :] + np.eye(degree + 1)
    matrix = values[:, None] / values[None, :] / differ
    matrix = matrix * (1.0 - np.eye(degree + 1))
    matrix[0, 0] = -degree * (degree + 1) / 4.0
    matrix[degree, degree] = degree * (degree + 1) / 4.0
    twice = 2.0 * matrix
    half = np.arange(128) // 64
    along = np.zeros((4, 4, 2, 128))
    for t in range(4):
        for source in range(4):
            along[t, source, 0] = twice[2 * t + half, 2 * source + half]
            along[t, source, 1] = twice[2 * t + half, 2 * source + 1 - half]
    rows = np.stack([np.tile(np.repeat(twice.T, 8, axis=1), 2), np.tile(twice.T, 16)]).astype(np.float32)
    high = rows.astype(BF16)
    low = (rows - high.astype(np.float32)).astype(BF16)
    parts = [along.reshape(32, 128), *high, *low]
    return np.concatenate([part.astype(np.float32) for part in parts])


def along_slope(x, rows_ref):
    turned = [pltpu.roll(value, 64, 1) for value in x]
    slopes = []
    for t in range(4):
        slope = None
        for s in range(4):
            n = 8 * t + 2 * s
            term = rows_ref[n : n + 1, :] * x[s] + rows_ref[n + 1 : n + 2, :] * turned[s]
            slope = term if slope is None else slope + term
        slopes.append(slope)
    return slopes


def fill_table(rows_ref, table):
    lane = lanes((16, 128))
    sub = lax.broadcasted_iota(jnp.int32, (16, 128), 0)
    zero = jnp.zeros((16, 128), F32)
    table[...] = jnp.zeros((2, 512, 256), BF16)
    for h in range(2):
        base = 32 + 16 * h
        row = rows_ref[base + 8 : base + 16, :]
        vertical = jnp.concatenate([row, row], axis=0)
        for g in range(16):
            here = tile(g // 8)
            j = base + 2 * g % 8
            row = jnp.where(sub >= 8, rows_ref[j + 1 : j + 2, :], rows_ref[j : j + 1, :])
            inside = ((lane >> 6) == g // 4 % 2) & ((lane & 7) == (sub & 7))
            table[h, 16 * g : 16 * g + 16, here] = jnp.where(inside, row, zero).astype(BF16)
            inside = (lane >> 3) == (sub >> 3) + 2 * (g % 8)
            table[h, 256 + 16 * g : 272 + 16 * g, here] = jnp.where(inside, vertical, zero).astype(BF16)


def split(x):
    high = x.astype(BF16)
    return high, (x - high.astype(F32)).astype(BF16)


def product(high, low, table_high, table_low):
    def dot(a, b):
        return jnp.dot(a, b, preferred_element_type=F32)

    return dot(high, table_high) + (dot(low, table_high) + dot(high, table_low))


def lanes(shape):
    return lax.broadcasted_iota(jnp.int32, shape, len(shape) - 1)


def tile(t):
    return slice(128 * t, 128 * t + 128)


def is_even(axis):
    return (lax.axis_index(axis) & 1) == 0


def holder_kernel(
    slot_hbm, store_hbm, rows_hbm,
    out_hbm,
    slot_ref, store_ref, rows_ref, table, stage, high, low, total, sems,
):
    pieces = [
        (slot_hbm, slot_ref),
        (store_hbm, store_ref),
        (rows_hbm, rows_ref),
    ]
    copies = [pltpu.make_async_copy(src, dst, sems.at[n]) for n, (src, dst) in enumerate(pieces)]
    for copy in copies:
        copy.start()
    copies[2].wait()
    fill_table(rows_ref, table)
    copies[0].wait()
    copies[1].wait()

    for g in range(16):
        rows = slice(16 * g, 16 * g + 16)
        for m in range(4):
            slot = slot_ref[2 * PEER_ORDER[2 * g + m // 2] + m % 2]
            for f in range(3):
                stage[f, g, 4 * m : 4 * m + 4, :] = store_ref[slot, f]
        slopes = along_slope([stage[0, g, :, tile(t)] for t in range(4)], rows_ref)
        for t in range(4):
            total[slice(2 * g, 2 * g + 2), :, tile(t)] = slopes[t].reshape(2, 8, 128)
        for f in range(2):
            high[f, rows], low[f, rows] = split(stage[f + 1, g])
    writes = []
    for c in range(2):
        part = slice(256 * c, 256 * c + 256)
        spread = product(high[0, :, part], low[0, :, part], table[0, 0:256], table[1, 0:256])
        spread += product(high[1, :, part], low[1, :, part], table[0, 256:512], table[1, 256:512])
        total[:, :, part] += spread.reshape(32, 8, 256)
        writes.append(
            pltpu.make_async_copy(total.at[:, :, part], out_hbm.at[:, :, part], sems.at[3 + c])
        )
        writes[c].start()
    for write in writes:
        write.wait()


def trace_kernel(adj_ref, along_one, along_two, cross_one, cross_two):
    even = is_even("along")
    for f in range(4):
        for c in range(4):
            rows = slice(4 * c, 4 * c + 4)
            first = adj_ref[f, 0, c, :, tile(0)]
            last = adj_ref[f, 7, c, :, tile(3)]
            along_one[f, rows, :] = jnp.where(even, last, first)
            along_two[f, rows, :] = jnp.where(even, first, last)
    even = is_even("cross")
    j = (lanes((4, 128)) >> 3) & 7
    for f in range(4):
        for t in range(4):
            last = pltpu.roll(adj_ref[f, 0, 3, :, tile(t)], 72, 1)
            first = adj_ref[f, 0, 0, :, tile(t)]
            for a in range(1, 8):
                other = adj_ref[f, a, 3, :, tile(t)]
                last = jnp.where(j == a, pltpu.roll(other, (72 + 8 * a) % 128, 1), last)
                other = adj_ref[f, a, 0, :, tile(t)]
                first = jnp.where(j == a, pltpu.roll(other, 8 * a, 1), first)
            cross_one[f, :, tile(t)] = jnp.where(even, last, first)
            cross_two[f, :, tile(t)] = jnp.where(even, first, last)


def volume_kernel(
    node_ref, residual_ref, adj_ref, rows_ref, out_ref, table, state, high, low, slope_x, slope_y, slope_z, ground
):
    fill_table(rows_ref, table)
    row = {2: 0, 0: 128, 3: 256}
    state[:, 0] = jnp.zeros((4, 16, 512), F32)
    state[:, 9] = jnp.zeros((4, 16, 512), F32)

    def load(a, carry):
        for f in range(4):
            for c in range(4):
                state[f, a + 1, 4 * c : 4 * c + 4, :] = adj_ref[f, a, c]
            slopes = along_slope([state[f, a + 1, :, tile(t)] for t in range(4)], rows_ref)
            for t in range(4):
                slope_x[f, a, :, tile(t)] = slopes[t]
            if f in row:
                rows = pl.ds(pl.multiple_of(row[f] + a * 16, 16), 16)
                high[rows], low[rows] = split(state[f, a + 1])
        return carry

    lax.fori_loop(0, 8, load, 0, unroll=8)
    for c in range(2):
        part = slice(256 * c, 256 * c + 256)
        slope_y[:, part] = product(high[0:256, part], low[0:256, part], table[0, 0:256], table[1, 0:256])
        slope_z[:, part] = product(
            high[128:384, part], low[128:384, part], table[0, 256:512], table[1, 256:512]
        )

    node = node_ref[...]
    residual = residual_ref[...]
    target = lax.broadcasted_iota(jnp.int32, (128, 128), 0)
    spread = jnp.where(target == 4 * (node >> 6), residual, 0.0)
    place = lax.broadcasted_iota(jnp.int32, (512, 128), 0) == 8 * (node & 63)
    place = jnp.where(place, 1.0, 0.0).astype(BF16)
    ones, rest = split(spread)
    twos = (spread - ones.astype(F32) - rest.astype(F32)).astype(BF16)

    def match(a):
        return lax.dot_general(a, place, (((1,), (1,)), ((), ())), preferred_element_type=F32)

    ground[...] = match(ones) + (match(rest) + match(twos))

    lane = lanes((8, 128))
    sub = lax.broadcasted_iota(jnp.int32, (8, 128), 0)
    j = (lane >> 3) & 7
    k = lane & 7
    e = sub & 3
    odd = sub >= 4
    top_y = j == 7
    top_z = k == 7
    floor = e == 0
    ceiling = e == 3
    zero = jnp.zeros((8, 128), F32)
    sign_y = jnp.where(j == 0, HALF_LIFT, jnp.where(top_y, -HALF_LIFT, 0.0))
    size_y = jnp.where((j == 0) | top_y, -HALF_LIFT * ALPHA, 0.0)
    sign_z = jnp.where(k == 0, HALF_LIFT, jnp.where(top_z, -HALF_LIFT, 0.0))
    size_z = jnp.where((k == 0) | top_z, -HALF_LIFT * ALPHA, 0.0)

    def step(a, carry):
        for t in range(4):
            here = tile(t)
            q = [[state[f, a + 1, 8 * g : 8 * g + 8, here] for g in range(2)] for f in range(4)]
            dy = [[None] * 2 for _ in range(4)]
            dz = [[None] * 2 for _ in range(4)]
            dx = [[None] * 2 for _ in range(4)]
            for f in range(4):
                swap = [pltpu.roll(q[f][g], 4, 0) for g in range(2)]
                before = [jnp.where(odd, swap[0], zero), jnp.where(odd, swap[1], swap[0])]
                after = [jnp.where(odd, swap[1], swap[0]), jnp.where(odd, zero, swap[1])]
                for g in range(2):
                    x = q[f][g]
                    outer = jnp.where(top_y, pltpu.roll(after[g], 56, 1), pltpu.roll(before[g], 72, 1))
                    dy[f][g] = x - outer
                    below = pltpu.roll(pltpu.roll(x, 1, 0), 121, 1)
                    below = jnp.where(floor, -x if f == 3 else x, below)
                    above = pltpu.roll(pltpu.roll(x, 7, 0), 7, 1)
                    above = jnp.where(ceiling, zero, above)
                    dz[f][g] = x - jnp.where(top_z, above, below)
                    if t == 0:
                        outer = pltpu.roll(state[f, a, 8 * g : 8 * g + 8, tile(3)], 64, 1)
                        dx[f][g] = jnp.where(lane < 64, x - outer, zero)
                    if t == 3:
                        outer = pltpu.roll(state[f, a + 2, 8 * g : 8 * g + 8, tile(0)], 64, 1)
                        dx[f][g] = jnp.where(lane >= 64, x - outer, zero)
            for g in range(2):
                def rows(f, base=0):
                    return pl.ds(pl.multiple_of(row[f] - base + a * 16 + 8 * g, 8), 8)

                gx = [slope_x[f, a, 8 * g : 8 * g + 8, here] for f in range(4)]
                gy = {f: slope_y[rows(f), here] for f in (2, 0)}
                gz = {f: slope_z[rows(f, 128), here] for f in (0, 3)}
                rate = [
                    MACH * gx[0] + gx[1] + gy[2] + gz[3],
                    MACH * gx[1] + gx[0],
                    MACH * gx[2] + gy[0],
                    MACH * gx[3] + gz[0],
                ]
                for f in range(4):
                    rate[f] = rate[f] + size_y * dy[f][g] + size_z * dz[f][g]
                rate[0] = rate[0] + sign_y * dy[2][g] + sign_z * dz[3][g]
                rate[2] = rate[2] + sign_y * dy[0][g]
                rate[3] = rate[3] + sign_z * dz[0][g]
                if t in (0, 3):
                    s = -1.0 if t == 0 else 1.0
                    d = [dx[f][g] for f in range(4)]
                    own = -HALF_LIFT * (s * MACH + ALPHA)
                    rate[0] = rate[0] + own * d[0] - (HALF_LIFT * s) * d[1]
                    rate[1] = rate[1] + own * d[1] - (HALF_LIFT * s) * d[0]
                    rate[2] = rate[2] + own * d[2]
                    rate[3] = rate[3] + own * d[3]
                new = [q[f][g] + TIME_STEP * rate[f] for f in range(4)]
                source = ground[pl.ds(pl.multiple_of(a * 16 + 8 * g, 8), 8), here]
                new[0] = new[0] + (TIME_STEP * SOURCE_GAIN) * source
                for f in range(4):
                    out_ref[f, a, 8 * g : 8 * g + 8, here] = new[f]
        return carry

    lax.fori_loop(0, 8, step, 0, unroll=8)


def finish_kernel(
    arrival_ref, adj_ref, new_ref, cross_two, along_two, cross_one, along_one, received_ref,
    next_hbm, kappa_hbm, next_ref, kappa_ref, edge, side, place, sems,
):
    for n, peer in enumerate(PEER_ORDER):
        place[peer] = n
    lift = TIME_STEP * HALF_LIFT
    lane = lanes((4, 128))
    j = (lane >> 3) & 7

    def arrived(axis, one, two, s, f, index):
        use_one = is_even(axis) if s > 0 else jnp.logical_not(is_even(axis))
        return jnp.where(use_one, one[(f, *index)], two[(f, *index)])

    def along_terms(s, rows):
        q = [arrived("along", along_one, along_two, s, f, (rows, slice(None))) for f in range(4)]
        q = [pltpu.roll(x, 64, 1) for x in q]
        own = lift * (s * MACH + ALPHA)
        return [own * q[0] + (lift * s) * q[1], own * q[1] + (lift * s) * q[0], own * q[2], own * q[3]]

    def cross_terms(s, t):
        q = [arrived("cross", cross_one, cross_two, s, f, (slice(None), tile(t))) for f in range(4)]
        own = lift * ALPHA
        return [
            own * q[0] + (lift * s) * q[2], own * q[1], own * q[2] + (lift * s) * q[0], own * q[3],
        ]

    for c in range(4):
        rows = slice(4 * c, 4 * c + 4)
        low = along_terms(-1.0, rows)
        high = along_terms(1.0, rows)
        for f in range(4):
            edge[0, f, rows, :] = jnp.where(lane < 64, low[f], 0.0)
            edge[1, f, rows, :] = jnp.where(lane >= 64, high[f], 0.0)
    for t in range(4):
        low = cross_terms(-1.0, t)
        high = cross_terms(1.0, t)
        for f in range(4):
            side[0, f, :, tile(t)] = low[f]
            side[1, f, :, tile(t)] = high[f]
    writes = []
    for f in range(4):
        for t in range(4):
            for a in range(8):
                for c in range(4):
                    value = new_ref[f, a, 4 * c : 4 * c + 4, tile(t)]
                    if c == 0:
                        beyond = pltpu.roll(side[0, f, :, tile(t)], (128 - 8 * a) % 128, 1)
                        value = value + jnp.where(j == 0, beyond, 0.0)
                    if c == 3:
                        beyond = pltpu.roll(side[1, f, :, tile(t)], (56 - 8 * a) % 128, 1)
                        value = value + jnp.where(j == 7, beyond, 0.0)
                    if t == 0 and a == 0:
                        value = value + edge[0, f, 4 * c : 4 * c + 4, :]
                    if t == 3 and a == 7:
                        value = value + edge[1, f, 4 * c : 4 * c + 4, :]
                    next_ref[f, a, c, :, tile(t)] = value
        if f % 2 == 1:
            pair = slice(f - 1, f + 1)
            writes.append(pltpu.make_async_copy(next_ref.at[pair], next_hbm.at[pair], sems.at[f]))
            writes[-1].start()
    for a in range(8):
        for c in range(4):
            q = arrival_ref[a, c]
            clipped = jnp.maximum(q, 0)
            holder = place[clipped >> 1]
            second = (clipped & 1) == 1
            block = jnp.where(second, received_ref[holder, 4:8, :], received_ref[holder, 0:4, :])
            value = TIME_STEP * adj_ref[0, a, c] * block
            kappa_ref[a, c] = jnp.where(q >= 0, value, 0.0)
    writes.append(pltpu.make_async_copy(kappa_ref, kappa_hbm, sems.at[4]))
    writes[-1].start()
    for write in writes:
        write.wait()


VMEM = pl.BlockSpec(memory_space=pltpu.VMEM)
HBM = pl.BlockSpec(memory_space=pltpu.HBM)
SMEM = pl.BlockSpec(memory_space=pltpu.SMEM)


def kernel(body, out_shape, in_specs, scratch, flops, moved, out_specs=None, limit=VMEM_BYTES):
    return pl.pallas_call(
        body,
        out_shape=out_shape,
        in_specs=in_specs,
        out_specs=out_specs or jax.tree.map(lambda _: VMEM, out_shape),
        scratch_shapes=scratch,
        compiler_params=pltpu.CompilerParams(vmem_limit_bytes=limit),
        cost_estimate=pl.CostEstimate(flops=flops, bytes_accessed=moved, transcendentals=0),
    )


def array(*shape):
    return jax.ShapeDtypeStruct(shape, F32)


def exchange(value, axis, start):
    pairs = []
    for i in range(start, lax.axis_size(axis) - 1, 2):
        pairs += [(i, i + 1), (i + 1, i)]
    return lax.ppermute(value, axis, pairs)


def per_device(adjoint_state, snapshot_store, dispatch_slot, arrival_slot, mic_node, mic_residual):
    rows = jnp.asarray(derivative_rows())
    outgoing = kernel(
        holder_kernel,
        array(32, 8, 512),
        [HBM] * 3,
        [
            pltpu.SMEM((64,), jnp.int32),
            pltpu.VMEM((64, 3, 4, 512), F32),
            pltpu.VMEM((64, 128), F32),
            pltpu.VMEM((2, 512, 256), BF16),
            pltpu.VMEM((3, 16, 16, 512), F32),
            pltpu.VMEM((2, 256, 512), BF16),
            pltpu.VMEM((2, 256, 512), BF16),
            pltpu.VMEM((32, 8, 512), F32),
            pltpu.SemaphoreType.DMA((5,)),
        ],
        3_000_000_000, 5_000_000,
        HBM,
        HOLDER_BYTES,
    )(dispatch_slot, snapshot_store, rows)
    received = lax.all_to_all(
        outgoing, "cross", split_axis=0, concat_axis=0, axis_index_groups=[list(PEER_ORDER)], tiled=True
    )
    along_one, along_two, cross_one, cross_two = kernel(
        trace_kernel,
        (array(4, 16, 128), array(4, 16, 128), array(4, 4, 512), array(4, 4, 512)),
        [VMEM],
        [],
        1_000_000, 500_000,
    )(adjoint_state)
    updated = kernel(
        volume_kernel,
        array(4, 8, 16, 512),
        [VMEM] * 4,
        [
            pltpu.VMEM((2, 512, 256), BF16),
            pltpu.VMEM((4, 10, 16, 512), F32),
            pltpu.VMEM((384, 512), BF16),
            pltpu.VMEM((384, 512), BF16),
            pltpu.VMEM((4, 8, 16, 512), F32),
            pltpu.VMEM((256, 512), F32),
            pltpu.VMEM((256, 512), F32),
            pltpu.VMEM((128, 512), F32),
        ],
        4_000_000_000, 4_000_000,
    )(mic_node.reshape(1, 128), mic_residual.reshape(1, 128), adjoint_state, rows)
    along_one = exchange(along_one, "along", 0)
    along_two = exchange(along_two, "along", 1)
    cross_one = exchange(cross_one, "cross", 0)
    cross_two = exchange(cross_two, "cross", 1)
    return kernel(
        finish_kernel,
        (array(4, 8, 4, 4, 512), array(8, 4, 4, 512)),
        [SMEM] + [VMEM] * 7,
        [
            pltpu.VMEM((4, 8, 4, 4, 512), F32),
            pltpu.VMEM((8, 4, 4, 512), F32),
            pltpu.VMEM((2, 4, 16, 128), F32),
            pltpu.VMEM((2, 4, 4, 512), F32),
            pltpu.SMEM((32,), jnp.int32),
            pltpu.SemaphoreType.DMA((5,)),
        ],
        10_000_000, 4_000_000,
        (HBM, HBM),
    )(
        arrival_slot, adjoint_state, updated, cross_two, along_two, cross_one, along_one, received
    )


def solution(mesh):
    in_specs = (
        P(None, "along", "cross", None, None),
        P(("along", "cross"), None, None, None),
        P(("along", "cross")),
        P("along", "cross"),
        P(("along", "cross")),
        P(("along", "cross")),
    )
    out_specs = (P(None, "along", "cross", None, None), P("along", "cross", None, None))
    return jax.shard_map(
        per_device, mesh=mesh, in_specs=in_specs, out_specs=out_specs, check_vma=False
    )
```
